32 devices in a mesh: row: 2 (over x), col: 4 (over y, core), item: 4 (over z).
Axes of the slice: x: 2, y: 2, z: 4, core: 2. Of those that a mesh axis runs over, the one named last changes fastest.
Arguments:
- tokens: bfloat16 [4, 2, 64, 2432], P('item', 'row', 'col'), may hold values from -6 to 6
- text_keys_values: bfloat16 [4, 154, 2, 2048], P('item', None, None, 'row'), may hold values from -200 to 200
- text_length: int32 [4], P('item'), may hold values from 2 to 154, as said below
- modulation: float32 [4, 8, 2432], P('item'), may hold values from -4 to 4
- input_weight: bfloat16 [2432, 3, 2048], P(None, None, 'row'), may hold values from -0.125 to 0.125
- norm_gain: float32 [2, 64], replicated, may hold values from 1 to 3
- output_weight: bfloat16 [2048, 2432], P('row'), may hold values from -0.125 to 0.125
- up_weight: bfloat16 [2432, 9728], P(None, 'row'), may hold values from -0.125 to 0.125
- down_weight: bfloat16 [9728, 2432], P('row'), may hold values from -0.0625 to 0.0625
- final_weight: bfloat16 [2432, 64], replicated, may hold values from -0.125 to 0.125
- step_index: int32 [1], replicated, may hold values from 0 to 27
- latent: float32 [4, 2, 4096], P('item', 'row', 'col'), may hold values from -6 to 6
Outputs:
- tokens_out: bfloat16 [4, 2, 64, 2432], P('item', 'row', 'col')
- velocity: float32 [4, 2, 4096], P('item', 'row', 'col')
- latent_next: float32 [4, 2, 4096], P('item', 'row', 'col')
The draws below stay inside these ranges and needn't reach their ends.
Inputs may be any that keep to these rules, and one draw needn't show every extreme that they name: `text_length`: at least one sequence has all 154 text tokens valid.
All inputs are finite; a program needn't handle non-finite values.
Results may differ from the reference program's by a relative error of at most 0.024.
Values may be sent and summed in bfloat16 or wider, within the bound.
No kernel may reach another device: no remote copies, remote signals or barrier semaphores. Data moves between devices by JAX's collectives and lax.ppermute only.
A program may use at most 128 MiB of HBM per device.

```python
import math
import jax
import jax.numpy as jnp
from jax import lax

D = 2432
HEADS = 32
HD = 64
FF = 9728
PC = 64
TXT = 154
STEPS = 28
GH = 2
GW = 64
IMG = 128
SEQS = 4
N_ROW = 2


def draw_text_length(key, part):
    lengths = jax.random.randint(key, (SEQS,), 2, TXT + 1)
    chosen = jax.random.randint(jax.random.fold_in(key, 7), (), 0, SEQS)
    return jnp.where(jnp.arange(SEQS) == chosen, TXT, lengths).astype(jnp.int32)


def draw_text_keys_values(key, part):
    sampled = jnp.clip(jax.random.normal(key, (SEQS, TXT, 2, HEADS * HD), jnp.float32), -6.0, 6.0) * 2.5
    return sampled.astype(jnp.bfloat16)


def steps_of(own_key, dims, shards, least, high):
    gain = 1.0
    for axis_at, shards_of in shards:
        steps = jax.random.uniform(jax.random.fold_in(jax.random.fold_in(own_key, 6), axis_at), (shards_of,), jnp.float32, least / len(shards), high / len(shards))
        gain = gain * jnp.repeat(jnp.exp(steps), dims[axis_at] // shards_of).reshape((-1,) + (1,) * (len(dims) - 1 - axis_at))
    return gain


def noise(rng, extent, deviation, limit, pieces=(), kind=jnp.bfloat16):
    factor_of = steps_of(rng, extent, pieces, -0.22, 0.18) if pieces else 1.0
    drawn = jax.random.normal(rng, extent, jnp.float32) * deviation * factor_of
    return jnp.minimum(jnp.maximum(drawn, -limit), limit).astype(kind)


def setup_inputs(seed: int = 0) -> dict:
    key_list = jax.random.split(jax.random.key(seed), 13)
    return {
        "tokens": noise(key_list[0], (SEQS, GH, GW, D), 1.0, 6.0, ((0, 4), (1, 2), (2, 4))),
        "text_keys_values": draw_text_keys_values(jax.random.fold_in(key_list[12], 71), 0),
        "text_length": draw_text_length(jax.random.fold_in(key_list[12], 71), 0),
        "modulation": noise(key_list[3], (SEQS, 8, D), 0.7, 4.0, ((0, 4),), jnp.float32),
        "input_weight": noise(key_list[4], (D, 3, HEADS * HD), D ** -0.5, 0.125, ((2, 2),)),
        "norm_gain": jnp.clip(jnp.exp(jax.random.uniform(key_list[5], (2, HD), jnp.float32, math.log(1.0), math.log(3.0))), 1.0, 3.0),
        "output_weight": noise(key_list[6], (HEADS * HD, D), (HEADS * HD) ** -0.5, 0.125, ((0, 2),)),
        "up_weight": noise(key_list[7], (D, FF), D ** -0.5, 0.125, ((1, 2),)),
        "down_weight": noise(key_list[8], (FF, D), FF ** -0.5, 0.0625, ((0, 2),)),
        "final_weight": noise(key_list[9], (D, PC), D ** -0.5, 0.125),
        "step_index": jax.random.randint(key_list[10], (1,), 0, STEPS).astype(jnp.int32),
        "latent": noise(key_list[11], (SEQS, GH, GW * PC), 1.0, 6.0, ((0, 4), (1, 2), (2, 4)), jnp.float32),
    }


EPSILON = 1e-06
SHIFT_FACTOR = 3.0
GUIDANCE = 4.5
MASKED = -1e+30

def layer_norm(values):
    center = values - lax.optimization_barrier(jnp.mean(values, axis=-1, keepdims=True))
    spread = lax.optimization_barrier(jnp.mean(center * center, axis=-1, keepdims=True))
    return center * lax.rsqrt(spread + EPSILON)

def modulate(values, shift_term, scale_term):
    return (layer_norm(values) * (1.0 + scale_term) + shift_term).astype(jnp.bfloat16)

def root_norm(values, gain_row):
    return values * lax.rsqrt(lax.optimization_barrier(jnp.mean(values * values, axis=-1, keepdims=True)) + EPSILON) * gain_row

def noise_level(position):
    linear = 1.0 - position / STEPS
    return SHIFT_FACTOR * linear / (1.0 + (SHIFT_FACTOR - 1.0) * linear)

def one_sequence(tile_grid, text_pairs, length, mod_rows, input_weight, norm_gain, output_weight, up_weight, down_weight, final_weight):
    states = tile_grid.reshape(IMG, D).astype(jnp.float32)
    attn_input = modulate(states, mod_rows[0], mod_rows[1])
    projected = jnp.dot(attn_input, input_weight.reshape(D, 3 * HEADS * HD), preferred_element_type=jnp.float32)
    projected = projected.reshape(IMG, 3, HEADS, HD)
    queries = root_norm(projected[:, 0], norm_gain[0]).astype(jnp.bfloat16)
    keys_image = root_norm(projected[:, 1], norm_gain[1]).astype(jnp.bfloat16)
    values_image = projected[:, 2].astype(jnp.bfloat16)
    keys_text = text_pairs[:, 0].reshape(TXT, HEADS, HD)
    values_text = text_pairs[:, 1].reshape(TXT, HEADS, HD)
    keep_mask = jnp.concatenate([jnp.ones((IMG,), dtype=bool), jnp.arange(TXT) < length])
    all_keys = jnp.concatenate([keys_image, keys_text], axis=0)
    all_values = jnp.concatenate([values_image, values_text], axis=0)

    def attend(head_index):
        query_head = queries[:, head_index]
        key_head = all_keys[:, head_index]
        value_head = all_values[:, head_index]
        scores = jnp.dot(query_head, key_head.T, preferred_element_type=jnp.float32) * HD ** (-0.5)
        scores = jnp.where(keep_mask[None, :], scores, MASKED)
        largest = lax.optimization_barrier(jnp.max(scores, axis=1, keepdims=True))
        weights = jnp.exp(scores - largest)
        total_mass = lax.optimization_barrier(jnp.sum(weights, axis=1, keepdims=True))
        mixture = jnp.dot(weights.astype(jnp.bfloat16), value_head, preferred_element_type=jnp.float32)
        return (mixture / total_mass).astype(jnp.bfloat16)
    heads_out = lax.map(attend, jnp.arange(HEADS))
    attended = heads_out.transpose(1, 0, 2).reshape(IMG, HEADS * HD)
    group_width = HEADS * HD // N_ROW
    attention = jnp.zeros((IMG, D), jnp.float32)
    for group_index in range(N_ROW):
        low = group_index * group_width
        partial_value = jnp.dot(attended[:, low:low + group_width], output_weight[low:low + group_width], preferred_element_type=jnp.float32)
        attention = attention + lax.optimization_barrier(partial_value.astype(jnp.bfloat16)).astype(jnp.float32)
    middle = states + mod_rows[2] * attention
    feed_input = modulate(middle, mod_rows[3], mod_rows[4])
    hidden = jax.nn.gelu(jnp.dot(feed_input, up_weight, preferred_element_type=jnp.float32), approximate=True).astype(jnp.bfloat16)
    hidden_width = FF // N_ROW
    feed = jnp.zeros((IMG, D), jnp.float32)
    for group_index in range(N_ROW):
        low = group_index * hidden_width
        partial_value = jnp.dot(hidden[:, low:low + hidden_width], down_weight[low:low + hidden_width], preferred_element_type=jnp.float32)
        feed = feed + lax.optimization_barrier(partial_value.astype(jnp.bfloat16)).astype(jnp.float32)
    leaving = middle + mod_rows[5] * feed
    final_input = modulate(leaving, mod_rows[6], mod_rows[7])
    raw_velocity = jnp.dot(final_input, final_weight, preferred_element_type=jnp.float32).reshape(GH, GW * PC)
    return (leaving.astype(jnp.bfloat16).reshape(GH, GW, D), raw_velocity)

def reference(tokens, text_keys_values, text_length, modulation, input_weight, norm_gain, output_weight, up_weight, down_weight, final_weight, step_index, latent):
    outputs = []
    velocities = []
    for sequence in range(SEQS):
        leaving, raw_velocity = one_sequence(tokens[sequence], text_keys_values[sequence], text_length[sequence], modulation[sequence], input_weight, norm_gain, output_weight, up_weight, down_weight, final_weight)
        outputs.append(leaving)
        velocities.append(raw_velocity)
    stacked = jnp.stack(velocities).reshape(SEQS // 2, 2, GH, GW * PC)
    guided = stacked[:, 0]
    unguided = stacked[:, 1]
    combined = unguided + GUIDANCE * (guided - unguided)
    velocity = jnp.stack([combined, combined], axis=1).reshape(SEQS, GH, GW * PC)
    position = step_index[0].astype(jnp.float32)
    step_size = noise_level(position + 1.0) - noise_level(position)
    return (jnp.stack(outputs), velocity, latent + step_size * velocity)
```

```python
import functools

import jax
import jax.numpy as jnp
from jax import lax
from jax.experimental import pallas as pl
from jax.experimental.pallas import tpu as pltpu
from jax.sharding import PartitionSpec as P

HD = 64
STEPS = 28

EPSILON = 1e-06
SHIFT_FACTOR = 3.0
GUIDANCE = 4.5
MASKED = -1e30

LANES = 128
TILE = 256
ROWS = 16
SCOPED = 12 << 20

IN_VMEM = pl.BlockSpec(memory_space=pltpu.VMEM)
IN_SMEM = pl.BlockSpec(memory_space=pltpu.SMEM)
IN_PLACE = pl.BlockSpec(memory_space=pl.ANY)


def noise_level(position):
    linear = 1.0 - position / STEPS
    return SHIFT_FACTOR * linear / (1.0 + (SHIFT_FACTOR - 1.0) * linear)


def layer_norm(values):
    center = values - jnp.mean(values, axis=-1, keepdims=True)
    spread = jnp.mean(center * center, axis=-1, keepdims=True)
    return center * lax.rsqrt(spread + EPSILON)


def modulated(values, mod_ref, shift_row, scale_row):
    scale = 1.0 + mod_ref[scale_row : scale_row + 1, :]
    shift = mod_ref[shift_row : shift_row + 1, :]
    return (layer_norm(values) * scale + shift).astype(jnp.bfloat16)


def spans(width, step):
    return [(low, min(step, width - low)) for low in range(0, width, step)]


def for_rows(rows, step, body):
    if rows <= 2 * LANES:
        for low in range(0, rows, step):
            body(low)
    else:
        pl.loop(0, rows // step)(lambda at: body(pl.multiple_of(at * step, step)))


def in_hbm(array):
    return pltpu.with_memory_space_constraint(array, pltpu.HBM)


def in_vmem(array):
    return pltpu.with_memory_space_constraint(array, pltpu.VMEM)


def bytes_of(arrays):
    return sum(a.size * a.dtype.itemsize for a in arrays)


def fetch_kernel(parts, *refs):
    sources = refs[: len(refs) - len(parts) - 1]
    targets = refs[len(sources) : -1]
    sems = refs[-1]
    copies = [
        pltpu.make_async_copy(sources[at].at[pl.ds(low, size)], target, sems.at[index])
        for index, ((at, low, size), target) in enumerate(zip(parts, targets))
    ]
    for copy in copies:
        copy.start()
    for copy in copies:
        copy.wait()


def fetch(sources, parts):
    shapes = [(size,) + sources[at].shape[1:] for at, low, size in parts]
    moved = sum(2 * functools.reduce(lambda a, b: a * b, shape) for shape in shapes)
    return pl.pallas_call(
        functools.partial(fetch_kernel, parts),
        out_shape=[pltpu.VMEM(shape, jnp.bfloat16) for shape in shapes],
        in_specs=[IN_PLACE] * len(sources),
        out_specs=[IN_VMEM] * len(parts),
        scratch_shapes=[pltpu.SemaphoreType.DMA((len(parts),))],
        compiler_params=pltpu.CompilerParams(vmem_limit_bytes=SCOPED),
        cost_estimate=pl.CostEstimate(flops=0, bytes_accessed=2 * moved, transcendentals=0),
    )(*[in_hbm(source) for source in sources])


def attention_kernel(n_blocks, own_rows, up_low, *refs):
    blocks = refs[:n_blocks]
    (length, mod, gains, text, in_w, out_w, up_hbm, out, up_part) = refs[n_blocks : n_blocks + 9]
    normed, q_ref, k_ref, v_ref, att_ref, sem = refs[n_blocks + 9 :]
    up_copy = pltpu.make_async_copy(up_hbm.at[pl.ds(up_low, up_part.shape[0])], up_part, sem)
    up_copy.start()

    all_rows, width = normed.shape
    local = in_w.shape[2]
    low = 0
    for block in blocks:

        def norm_rows(at, block=block, low=low):
            values = block[pl.ds(at, ROWS), :].astype(jnp.float32)
            normed[pl.ds(low + at, ROWS), :] = modulated(values, mod, 0, 1)

        for_rows(block.shape[0], ROWS, norm_rows)
        low += block.shape[0]

    tile = min(TILE, local)
    head_of_row = lax.broadcasted_iota(jnp.int32, (tile, tile), 0) // HD
    head_of_col = lax.broadcasted_iota(jnp.int32, (tile, tile), 1) // HD
    same_head = (head_of_row == head_of_col).astype(jnp.bfloat16)

    def head_norm(values, gain):
        squares = values * values
        high = squares.astype(jnp.bfloat16)
        rest = (squares - high.astype(jnp.float32)).astype(jnp.bfloat16)
        total = jnp.dot(high, same_head, preferred_element_type=jnp.float32)
        total += jnp.dot(rest, same_head, preferred_element_type=jnp.float32)
        return values * lax.rsqrt(total * (1.0 / HD) + EPSILON) * gain

    for at, size in spans(local, tile):
        cols = slice(at, at + size)

        def project(first, rows, part):
            return jnp.dot(
                normed[pl.ds(first, rows), :],
                in_w[part, :, cols],
                preferred_element_type=jnp.float32,
            )

        def keys_values(first):
            rows = min(LANES, all_rows)
            k_ref[pl.ds(first, rows), cols] = head_norm(
                project(first, rows, 1), gains[1:2, :size]
            ).astype(jnp.bfloat16)
            v_ref[pl.ds(first, rows), cols] = project(first, rows, 2).astype(jnp.bfloat16)

        def queries(first):
            rows = min(LANES, own_rows)
            q_ref[pl.ds(first, rows), cols] = head_norm(
                project(first, rows, 0), gains[0:1, :size]
            ).astype(jnp.bfloat16)

        for_rows(own_rows, min(LANES, own_rows), queries)
        for_rows(all_rows, min(LANES, all_rows), keys_values)

    text_rows = text.shape[1]
    used = lax.broadcasted_iota(jnp.int32, (1, text_rows), 1) < length[0]
    first_head = lax.broadcasted_iota(jnp.int32, (1, LANES), 1) < HD
    contract = (((1,), (1,)), ((), ()))
    for at, size in spans(local, LANES):
        cols = slice(at, at + size)
        q = q_ref[:, cols]
        zero = jnp.zeros_like(q)
        pair = jnp.concatenate([jnp.where(first_head, q, zero), jnp.where(first_head, zero, q)], 0)
        scores = HD ** (-0.5) * lax.dot_general(
            pair, k_ref[:, cols], contract, preferred_element_type=jnp.float32
        )
        text_scores = HD ** (-0.5) * lax.dot_general(
            pair, text[0, :, cols], contract, preferred_element_type=jnp.float32
        )
        text_scores = jnp.where(used, text_scores, MASKED)
        largest = jnp.maximum(
            jnp.max(scores, axis=-1, keepdims=True), jnp.max(text_scores, axis=-1, keepdims=True)
        )
        weights = jnp.exp(scores - largest)
        text_weights = jnp.exp(text_scores - largest)
        total = jnp.sum(weights, axis=-1, keepdims=True)
        total += jnp.sum(text_weights, axis=-1, keepdims=True)
        mixed = jnp.dot(
            weights.astype(jnp.bfloat16), v_ref[:, cols], preferred_element_type=jnp.float32
        )
        mixed += jnp.dot(
            text_weights.astype(jnp.bfloat16), text[1, :, cols], preferred_element_type=jnp.float32
        )
        mixed = mixed / total
        att_ref[:, cols] = jnp.where(first_head, mixed[:own_rows], mixed[own_rows:]).astype(
            jnp.bfloat16
        )

    for at, size in spans(width, TILE):
        cols = slice(at, at + size)
        out[:, cols] = jnp.dot(
            att_ref[...], out_w[:, cols], preferred_element_type=jnp.float32
        ).astype(jnp.bfloat16)
    up_copy.wait()


def attention_half(blocks, own_rows, length, mod, gains, text, in_w, out_w, up, up_low):
    width, local = mod.shape[1], in_w.shape[2]
    all_rows = sum(block.shape[0] for block in blocks)
    up_rows = up.shape[0] - up_low
    scoped = SCOPED if all_rows <= LANES else 48 << 20
    return pl.pallas_call(
        functools.partial(attention_kernel, len(blocks), own_rows, up_low),
        out_shape=[
            jax.ShapeDtypeStruct((own_rows, width), jnp.bfloat16),
            pltpu.VMEM((up_rows, up.shape[1]), jnp.bfloat16),
        ],
        in_specs=[IN_VMEM] * len(blocks) + [IN_SMEM] + [IN_VMEM] * 5 + [IN_PLACE],
        out_specs=[IN_VMEM] * 2,
        scratch_shapes=[
            pltpu.VMEM((all_rows, width), jnp.bfloat16),
            pltpu.VMEM((own_rows, local), jnp.bfloat16),
            pltpu.VMEM((all_rows, local), jnp.bfloat16),
            pltpu.VMEM((all_rows, local), jnp.bfloat16),
            pltpu.VMEM((own_rows, local), jnp.bfloat16),
            pltpu.SemaphoreType.DMA,
        ],
        compiler_params=pltpu.CompilerParams(vmem_limit_bytes=scoped),
    )(*blocks, length, mod, gains, text, in_vmem(in_w), in_vmem(out_w), in_hbm(up))


def feed_kernel(n_blocks, paired, n_up, n_down, down_low, *refs):
    blocks = refs[:n_blocks]
    mine, theirs, mod = refs[n_blocks : n_blocks + 3]
    ups = refs[n_blocks + 3 : n_blocks + 3 + n_up]
    at = n_blocks + 3 + n_up
    downs = refs[at : at + n_down]
    down_hbm = refs[at + n_down]
    out, middle, fed, hidden, down_last, sem = refs[at + n_down + 1 :]
    down_copy = pltpu.make_async_copy(
        down_hbm.at[pl.ds(down_low, down_last.shape[0])], down_last, sem
    )
    down_copy.start()

    rows, width = fed.shape
    low = 0
    for block in blocks:

        def norm_rows(at, block=block, low=low):
            here = low + at
            attention = mine[pl.ds(here, ROWS), :].astype(jnp.float32)
            if paired:
                there = (here + rows // 2) % rows
                attention += theirs[pl.ds(there, ROWS), :].astype(jnp.float32)
            values = block[pl.ds(at, ROWS), :].astype(jnp.float32) + mod[2:3, :] * attention
            middle[pl.ds(here, ROWS), :] = values
            fed[pl.ds(here, ROWS), :] = modulated(values, mod, 3, 4)

        for_rows(block.shape[0], ROWS, norm_rows)
        low += block.shape[0]

    for at, size in spans(hidden.shape[1], TILE):
        cols = slice(at, at + size)
        total, low = None, 0
        for up in ups:
            high = low + up.shape[0]
            part = jnp.dot(fed[:, low:high], up[:, cols], preferred_element_type=jnp.float32)
            total, low = part if total is None else total + part, high
        hidden[:, cols] = jax.nn.gelu(total, approximate=True).astype(jnp.bfloat16)

    down_copy.wait()
    for at, size in spans(width, TILE):
        cols = slice(at, at + size)
        total, low = None, 0
        for down in (*downs, down_last):
            high = low + down.shape[0]
            part = jnp.dot(hidden[:, low:high], down[:, cols], preferred_element_type=jnp.float32)
            total, low = part if total is None else total + part, high
        out[:, cols] = total.astype(jnp.bfloat16)


def feed_half(blocks, mine, theirs, paired, mod, ups, downs, down, down_low):
    rows, width = mine.shape
    scoped = SCOPED if rows <= LANES else 32 << 20
    return pl.pallas_call(
        functools.partial(feed_kernel, len(blocks), paired, len(ups), len(downs), down_low),
        out_shape=[
            jax.ShapeDtypeStruct((rows, width), jnp.bfloat16),
            jax.ShapeDtypeStruct((rows, width), jnp.float32),
        ],
        in_specs=[IN_VMEM] * (len(blocks) + 3 + len(ups) + len(downs)) + [IN_PLACE],
        out_specs=[IN_VMEM] * 2,
        scratch_shapes=[
            pltpu.VMEM((rows, width), jnp.bfloat16),
            pltpu.VMEM((rows, down.shape[0]), jnp.bfloat16),
            pltpu.VMEM((down.shape[0] - down_low, width), jnp.bfloat16),
            pltpu.SemaphoreType.DMA,
        ],
        compiler_params=pltpu.CompilerParams(vmem_limit_bytes=scoped),
    )(
        *blocks,
        mine,
        theirs,
        mod,
        *[in_vmem(up) for up in ups],
        *[in_vmem(down_part) for down_part in downs],
        in_hbm(down),
    )


def final_kernel(paired, middle, mine, theirs, mod, final_w, leaving_out, velocity):
    feed = mine[:ROWS, :].astype(jnp.float32)
    if paired:
        feed += theirs[...].astype(jnp.float32)
    leaving = middle[:ROWS, :] + mod[5:6, :] * feed
    leaving_out[...] = leaving.astype(jnp.bfloat16)
    velocity[...] = lax.dot_general(
        modulated(leaving, mod, 6, 7),
        final_w[...],
        (((1,), (1,)), ((), ())),
        preferred_element_type=jnp.float32,
    )


def final_step(middle, mine, theirs, paired, mod, final_w):
    width = mod.shape[1]
    return pl.pallas_call(
        functools.partial(final_kernel, paired),
        out_shape=[
            jax.ShapeDtypeStruct((ROWS, width), jnp.bfloat16),
            jax.ShapeDtypeStruct((ROWS, final_w.shape[0]), jnp.float32),
        ],
        in_specs=[IN_VMEM] * 5,
        out_specs=[IN_VMEM] * 2,
        compiler_params=pltpu.CompilerParams(vmem_limit_bytes=SCOPED),
    )(middle, mine, theirs, mod, final_w)


def flipped(value, axes, mask, count):
    return lax.ppermute(value, axes, [(source, source ^ mask) for source in range(count)])


def on_device(
    tokens,
    text_keys_values,
    text_length,
    modulation,
    input_weight,
    norm_gain,
    output_weight,
    up_weight,
    down_weight,
    final_weight,
    step_index,
    latent,
):
    n_row, n_col = lax.axis_size("row"), lax.axis_size("col")
    width = tokens.shape[3]
    tile = tokens.reshape(-1, width)
    local = input_weight.shape[2]
    mod = modulation[0]
    in_w = input_weight.transpose(1, 0, 2)
    paired = n_row == 2
    both = ("row", "col")
    count = n_row * n_col
    tile_rows = tile.shape[0]
    own_rows = n_row * tile_rows

    if paired and n_col == 4:
        near = [tile] + [flipped(tile, both, mask, count) for mask in (n_col, 2, n_col + 2)]
        in_vm, out_vm = fetch((in_w, output_weight), ((0, 0, 3), (1, 0, local)))
        near = list(lax.optimization_barrier((*near, in_vm, out_vm)))
        in_vm, out_vm = near[4:]
        near = near[:4]
        far = [flipped(part, both, 1, count) for part in near]
        blocks = near + far
    else:
        gathered = lax.all_gather(tile, ("col", "row"), axis=0, tiled=True)
        blocks = [jnp.roll(gathered, -lax.axis_index("col") * own_rows, axis=0)]
        in_vm, out_vm = fetch((in_w, output_weight), ((0, 0, 3), (1, 0, local)))
    up_low = width // 4 // LANES * LANES
    (up_first,) = fetch((up_weight,), ((0, 0, up_low),))

    text = jnp.pad(text_keys_values[0].transpose(1, 0, 2), ((0, 0), (0, -text_keys_values.shape[1] % ROWS), (0, 0)))
    gains = jnp.tile(norm_gain, (1, TILE // HD))
    mine, up_last = attention_half(
        blocks, own_rows, text_length, mod, gains, text, in_vm, out_vm, up_weight, up_low
    )
    if paired:
        theirs = flipped(mine, "row", 1, n_row)
        own_blocks = blocks[:2] if len(blocks) > 1 else [blocks[0][:own_rows]]
    else:
        mine = lax.psum(mine.astype(jnp.float32), "row")
        theirs = mine
        own_blocks = [blocks[0][:own_rows]]
    downs = fetch((down_weight,), ((0, 0, 3 * local), (0, 3 * local, local)))
    feed, middle = feed_half(
        own_blocks, mine, theirs, paired, mod, (up_first, up_last), downs, down_weight, 4 * local
    )
    if paired:
        fed_there = flipped(feed[tile_rows:], "row", 1, n_row)
    else:
        feed = lax.psum_scatter(feed.astype(jnp.float32), "row", scatter_dimension=0, tiled=True)
        fed_there = feed
        middle = lax.dynamic_slice_in_dim(
            middle, lax.axis_index("row") * tile_rows, tile_rows, 0
        )
    leaving, raw_velocity = final_step(middle, feed, fed_there, paired, mod, final_weight.T)
    raw_velocity = raw_velocity.reshape(latent.shape)
    partner = flipped(raw_velocity, "item", 1, lax.axis_size("item"))
    is_guided = lax.axis_index("item") % 2 == 0
    guided = jnp.where(is_guided, raw_velocity, partner)
    unguided = jnp.where(is_guided, partner, raw_velocity)
    velocity = unguided + GUIDANCE * (guided - unguided)
    position = step_index[0].astype(jnp.float32)
    step_size = noise_level(position + 1.0) - noise_level(position)
    return (leaving.reshape(tokens.shape), velocity, latent + step_size * velocity)


def solution(mesh):
    in_specs = (
        P("item", "row", "col", None),
        P("item", None, None, "row"),
        P("item"),
        P("item", None, None),
        P(None, None, "row"),
        P(),
        P("row", None),
        P(None, "row"),
        P("row", None),
        P(),
        P(),
        P("item", "row", "col"),
    )
    out_specs = (P("item", "row", "col", None), P("item", "row", "col"), P("item", "row", "col"))
    return jax.shard_map(
        on_device, mesh=mesh, in_specs=in_specs, out_specs=out_specs, check_vma=False
    )
```

```python
import functools

import jax
import jax.numpy as jnp
from jax import lax
from jax.experimental import pallas as pl
from jax.experimental.pallas import tpu as pltpu
from jax.sharding import PartitionSpec as P

HD = 64
STEPS = 28

EPSILON = 1e-06
SHIFT_FACTOR = 3.0
GUIDANCE = 4.5
MASKED = -1e30

LANES = 128
TILE = 256
ROWS = 16
SCOPED = 16 << 20
SCOPED_FETCH = 17 << 20

IN_VMEM = pl.BlockSpec(memory_space=pltpu.VMEM)
IN_SMEM = pl.BlockSpec(memory_space=pltpu.SMEM)
IN_PLACE = pl.BlockSpec(memory_space=pl.ANY)


def noise_level(position):
    linear = 1.0 - position / STEPS
    return SHIFT_FACTOR * linear / (1.0 + (SHIFT_FACTOR - 1.0) * linear)


def layer_norm(values):
    center = values - jnp.mean(values, axis=-1, keepdims=True)
    spread = jnp.mean(center * center, axis=-1, keepdims=True)
    return center * lax.rsqrt(spread + EPSILON)


def modulated(values, mod_ref, shift_row, scale_row):
    scale = 1.0 + mod_ref[scale_row : scale_row + 1, :]
    shift = mod_ref[shift_row : shift_row + 1, :]
    return (layer_norm(values) * scale + shift).astype(jnp.bfloat16)


def spans(width, step):
    return [(low, min(step, width - low)) for low in range(0, width, step)]


def for_rows(rows, step, body):
    if rows <= 2 * LANES:
        for low in range(0, rows, step):
            body(low)
    else:
        pl.loop(0, rows // step)(lambda at: body(pl.multiple_of(at * step, step)))


def in_hbm(array):
    return pltpu.with_memory_space_constraint(array, pltpu.HBM)


def in_vmem(array):
    return pltpu.with_memory_space_constraint(array, pltpu.VMEM)


def bytes_of(arrays):
    return sum(a.size * a.dtype.itemsize for a in arrays)


def fetch_kernel(parts, n_sources, *refs):
    sources = refs[:n_sources]
    targets = refs[-len(parts) - 2 : -2]
    done, sems = refs[-2:]
    done[...] = jnp.zeros_like(done)
    copies = [
        pltpu.make_async_copy(sources[at].at[pl.ds(low, size)], target, sems.at[index])
        for index, ((at, low, size), target) in enumerate(zip(parts, targets))
    ]
    for copy in copies:
        copy.start()
    for copy in copies:
        copy.wait()


def fetch(sources, parts, after=()):
    shapes = [(size,) + sources[at].shape[1:] for at, low, size in parts]
    moved = sum(2 * functools.reduce(lambda a, b: a * b, shape) for shape in shapes)
    return pl.pallas_call(
        functools.partial(fetch_kernel, parts, len(sources)),
        out_shape=[pltpu.VMEM(shape, jnp.bfloat16) for shape in shapes]
        + [jax.ShapeDtypeStruct((8, LANES), jnp.float32)],
        in_specs=[IN_PLACE] * (len(sources) + len(after)),
        out_specs=[IN_VMEM] * (len(parts) + 1),
        scratch_shapes=[pltpu.SemaphoreType.DMA((len(parts),))],
        compiler_params=pltpu.CompilerParams(vmem_limit_bytes=SCOPED_FETCH),
        cost_estimate=pl.CostEstimate(flops=0, bytes_accessed=2 * moved, transcendentals=0),
    )(*[in_hbm(source) for source in sources], *after)


def attention_kernel(n_blocks, own_rows, *refs):
    blocks = refs[:n_blocks]
    length, mod, gains, text, *in_ws, out_hbm, up_hbm = refs[n_blocks : n_blocks + 9]
    out, *ups = refs[n_blocks + 10 : -8]
    normed, q_ref, k_ref, v_ref, att_ref, out_w, out_sem, up_sems = refs[-8:]
    out_copy = pltpu.make_async_copy(out_hbm, out_w, out_sem)
    out_copy.start()
    up_copies, low = [], 0
    for at, up in enumerate(ups):
        rows = pl.ds(low, up.shape[0])
        up_copies.append(pltpu.make_async_copy(up_hbm.at[rows], up, up_sems.at[at]))
        up_copies[-1].start()
        low += up.shape[0]

    all_rows, width = normed.shape
    local = in_ws[0].shape[1]
    low = 0
    for block in blocks:

        def norm_rows(at, block=block, low=low):
            values = block[pl.ds(at, ROWS), :].astype(jnp.float32)
            normed[pl.ds(low + at, ROWS), :] = modulated(values, mod, 0, 1)

        for_rows(block.shape[0], ROWS, norm_rows)
        low += block.shape[0]

    tile = min(TILE, local)
    head_of_row = lax.broadcasted_iota(jnp.int32, (tile, tile), 0) // HD
    head_of_col = lax.broadcasted_iota(jnp.int32, (tile, tile), 1) // HD
    gain = jnp.concatenate([gains[...]] * (tile // HD), axis=1)
    same_head = (head_of_row == head_of_col).astype(jnp.bfloat16)

    def head_norm(values, gain_row):
        squares = values * values
        high = squares.astype(jnp.bfloat16)
        rest = (squares - high.astype(jnp.float32)).astype(jnp.bfloat16)
        total = jnp.dot(high, same_head, preferred_element_type=jnp.float32)
        total += jnp.dot(rest, same_head, preferred_element_type=jnp.float32)
        return values * lax.rsqrt(total * (1.0 / HD) + EPSILON) * gain_row

    for at, size in spans(local, tile):
        cols = slice(at, at + size)

        def project(first, rows, part):
            return jnp.dot(
                normed[pl.ds(first, rows), :],
                in_ws[part][:, cols],
                preferred_element_type=jnp.float32,
            )

        def keys_values(first):
            rows = min(LANES, all_rows)
            k_ref[pl.ds(first, rows), cols] = head_norm(
                project(first, rows, 1), gain[1:2, :size]
            ).astype(jnp.bfloat16)
            v_ref[pl.ds(first, rows), cols] = project(first, rows, 2).astype(jnp.bfloat16)

        def queries(first):
            rows = min(LANES, own_rows)
            q_ref[pl.ds(first, rows), cols] = head_norm(
                project(first, rows, 0), gain[0:1, :size]
            ).astype(jnp.bfloat16)

        for_rows(own_rows, min(LANES, own_rows), queries)
        for_rows(all_rows, min(LANES, all_rows), keys_values)

    text_rows = text.shape[1]
    used = lax.broadcasted_iota(jnp.int32, (1, text_rows), 1) < length[0]
    first_head = lax.broadcasted_iota(jnp.int32, (1, LANES), 1) < HD
    contract = (((1,), (1,)), ((), ()))
    for at, size in spans(local, LANES):
        cols = slice(at, at + size)
        q = q_ref[:, cols]
        zero = jnp.zeros_like(q)
        pair = jnp.concatenate([jnp.where(first_head, q, zero), jnp.where(first_head, zero, q)], 0)
        scores = HD ** (-0.5) * lax.dot_general(
            pair, k_ref[:, cols], contract, preferred_element_type=jnp.float32
        )
        text_scores = HD ** (-0.5) * lax.dot_general(
            pair, text[0, :, cols], contract, preferred_element_type=jnp.float32
        )
        text_scores = jnp.where(used, text_scores, MASKED)
        largest = jnp.maximum(
            jnp.max(scores, axis=-1, keepdims=True), jnp.max(text_scores, axis=-1, keepdims=True)
        )
        weights = jnp.exp(scores - largest)
        text_weights = jnp.exp(text_scores - largest)
        total = jnp.sum(weights, axis=-1, keepdims=True)
        total += jnp.sum(text_weights, axis=-1, keepdims=True)
        mixed = jnp.dot(
            weights.astype(jnp.bfloat16), v_ref[:, cols], preferred_element_type=jnp.float32
        )
        mixed += jnp.dot(
            text_weights.astype(jnp.bfloat16), text[1, :, cols], preferred_element_type=jnp.float32
        )
        mixed = mixed / total
        att_ref[:, cols] = jnp.where(first_head, mixed[:own_rows], mixed[own_rows:]).astype(
            jnp.bfloat16
        )

    out_copy.wait()
    for at, size in spans(width, TILE):
        cols = slice(at, at + size)
        out[:, cols] = jnp.dot(
            att_ref[...], out_w[:, cols], preferred_element_type=jnp.float32
        ).astype(jnp.bfloat16)
    for copy in up_copies:
        copy.wait()


def attention_half(blocks, own_rows, length, mod, gains, text, in_ws, out_w, up, up_rows, after):
    width, local = mod.shape[1], out_w.shape[0]
    all_rows = sum(block.shape[0] for block in blocks)
    scoped = SCOPED_FETCH if all_rows <= LANES else 48 << 20
    return pl.pallas_call(
        functools.partial(attention_kernel, len(blocks), own_rows),
        out_shape=[
            jax.ShapeDtypeStruct((own_rows, width), jnp.bfloat16),
            *[pltpu.VMEM((rows, up.shape[1]), jnp.bfloat16) for rows in up_rows],
        ],
        in_specs=[IN_VMEM] * len(blocks) + [IN_SMEM] + [IN_VMEM] * 6 + [IN_PLACE] * 3,
        out_specs=[IN_VMEM] * (1 + len(up_rows)),
        scratch_shapes=[
            pltpu.VMEM((all_rows, width), jnp.bfloat16),
            pltpu.VMEM((own_rows, local), jnp.bfloat16),
            pltpu.VMEM((all_rows, local), jnp.bfloat16),
            pltpu.VMEM((all_rows, local), jnp.bfloat16),
            pltpu.VMEM((own_rows, local), jnp.bfloat16),
            pltpu.VMEM((local, width), jnp.bfloat16),
            pltpu.SemaphoreType.DMA,
            pltpu.SemaphoreType.DMA((len(up_rows),)),
        ],
        compiler_params=pltpu.CompilerParams(vmem_limit_bytes=scoped),
    )(
        *blocks,
        length,
        mod,
        gains,
        text,
        *[in_vmem(part) for part in in_ws],
        in_hbm(out_w),
        in_hbm(up),
        after,
    )


def feed_kernel(n_blocks, n_ups, n_downs, paired, *refs):
    blocks = refs[:n_blocks]
    mine, theirs, mod = refs[n_blocks : n_blocks + 3]
    ups = refs[n_blocks + 3 : n_blocks + 3 + n_ups]
    downs = refs[n_blocks + 3 + n_ups : n_blocks + 3 + n_ups + n_downs]
    down_hbm, out, middle, fed, hidden, down_last, sem = refs[-7:]
    rows, width = fed.shape
    units, last = hidden.shape[1], down_last.shape[0]
    down_copy = pltpu.make_async_copy(down_hbm.at[pl.ds(units - last, last)], down_last, sem)
    down_copy.start()

    low = 0
    for block in blocks:

        def norm_rows(at, block=block, low=low):
            here = low + at
            attention = mine[pl.ds(here, ROWS), :].astype(jnp.float32)
            if paired:
                there = (here + rows // 2) % rows
                attention += theirs[pl.ds(there, ROWS), :].astype(jnp.float32)
            values = block[pl.ds(at, ROWS), :].astype(jnp.float32) + mod[2:3, :] * attention
            middle[pl.ds(here, ROWS), :] = values
            fed[pl.ds(here, ROWS), :] = modulated(values, mod, 3, 4)

        for_rows(block.shape[0], ROWS, norm_rows)
        low += block.shape[0]

    def product(left, parts, cols):
        sums, low = 0.0, 0
        for part in parts:
            here = slice(low, low + part.shape[0])
            sums += jnp.dot(left[:, here], part[:, cols], preferred_element_type=jnp.float32)
            low = here.stop
        return sums

    for at, size in spans(units, TILE):
        cols = slice(at, at + size)
        hidden[:, cols] = jax.nn.gelu(product(fed, ups, cols), approximate=True).astype(jnp.bfloat16)

    down_copy.wait()
    for at, size in spans(width, TILE):
        cols = slice(at, at + size)
        out[:, cols] = product(hidden, (*downs, down_last), cols).astype(jnp.bfloat16)


def feed_half(blocks, mine, theirs, paired, mod, ups, downs, down):
    rows, width = mine.shape
    units = down.shape[0]
    last = units - sum(part.shape[0] for part in downs)
    return pl.pallas_call(
        functools.partial(feed_kernel, len(blocks), len(ups), len(downs), paired),
        out_shape=[
            jax.ShapeDtypeStruct((rows, width), jnp.bfloat16),
            jax.ShapeDtypeStruct((rows, width), jnp.float32),
        ],
        in_specs=[IN_VMEM] * (len(blocks) + 3 + len(ups) + len(downs)) + [IN_PLACE],
        out_specs=[IN_VMEM] * 2,
        scratch_shapes=[
            pltpu.VMEM((rows, width), jnp.bfloat16),
            pltpu.VMEM((rows, units), jnp.bfloat16),
            pltpu.VMEM((last, width), jnp.bfloat16),
            pltpu.SemaphoreType.DMA,
        ],
        compiler_params=pltpu.CompilerParams(vmem_limit_bytes=SCOPED),
    )(*blocks, mine, theirs, mod, *[in_vmem(part) for part in (*ups, *downs)], in_hbm(down))


def final_kernel(paired, middle, mine, theirs, mod, final_w, leaving_out, velocity):
    feed = mine[:ROWS, :].astype(jnp.float32)
    if paired:
        feed += theirs[...].astype(jnp.float32)
    leaving = middle[:ROWS, :] + mod[5:6, :] * feed
    leaving_out[...] = leaving.astype(jnp.bfloat16)
    velocity[...] = lax.dot_general(
        modulated(leaving, mod, 6, 7),
        final_w[...],
        (((1,), (1,)), ((), ())),
        preferred_element_type=jnp.float32,
    )


def final_step(middle, mine, theirs, paired, mod, final_w):
    width = mod.shape[1]
    return pl.pallas_call(
        functools.partial(final_kernel, paired),
        out_shape=[
            jax.ShapeDtypeStruct((ROWS, width), jnp.bfloat16),
            jax.ShapeDtypeStruct((ROWS, final_w.shape[0]), jnp.float32),
        ],
        in_specs=[IN_VMEM] * 5,
        out_specs=[IN_VMEM] * 2,
        compiler_params=pltpu.CompilerParams(vmem_limit_bytes=SCOPED),
    )(middle, mine, theirs, mod, final_w)


def flipped(value, axes, mask, count):
    return lax.ppermute(value, axes, [(source, source ^ mask) for source in range(count)])


def on_device(
    tokens,
    text_keys_values,
    text_length,
    modulation,
    input_weight,
    norm_gain,
    output_weight,
    up_weight,
    down_weight,
    final_weight,
    step_index,
    latent,
):
    n_row, n_col = lax.axis_size("row"), lax.axis_size("col")
    width = tokens.shape[3]
    tile = tokens.reshape(-1, width)
    local = input_weight.shape[2]
    mod = modulation[0]
    in_w = input_weight.transpose(1, 0, 2).reshape(3 * width, local)
    paired = n_row == 2
    both = ("row", "col")
    count = n_row * n_col
    tile_rows = tile.shape[0]
    own_rows = n_row * tile_rows

    text = text_keys_values[0].transpose(1, 0, 2)
    text = jnp.pad(text, ((0, 0), (0, -text.shape[1] % ROWS), (0, 0)))

    thirds = [(0, part * width, width) for part in range(3)]
    if paired and n_col == 4:
        near = [tile] + [flipped(tile, both, mask, count) for mask in (n_col, 2, n_col + 2)]
        *in_ws, done = fetch((in_w,), thirds[:2], (text,))
        *near, done = lax.optimization_barrier((*near, done))
        blocks = near + [flipped(part, both, 1, count) for part in near]
    else:
        gathered = lax.all_gather(tile, ("col", "row"), axis=0, tiled=True)
        blocks = [jnp.roll(gathered, -lax.axis_index("col") * own_rows, axis=0)]
        *in_ws, done = fetch((in_w,), thirds[:2], (text,))
    in_last, done = fetch((in_w,), thirds[2:], (blocks[0], done))
    in_ws.append(in_last)
    step = 6 * LANES
    up_parts = spans(width, step)
    early = 2
    mine, *ups = attention_half(
        blocks,
        own_rows,
        text_length,
        mod,
        norm_gain,
        text,
        in_ws,
        output_weight,
        up_weight,
        [size for low, size in up_parts[:early]],
        done,
    )
    if paired:
        theirs = flipped(mine, "row", 1, n_row)
        own_blocks = blocks[:2] if len(blocks) > 1 else [blocks[0][:own_rows]]
    else:
        mine = lax.psum(mine.astype(jnp.float32), "row")
        theirs = mine
        own_blocks = [blocks[0][:own_rows]]
    edge = up_parts[early][0]
    late = [(0, edge + low, size) for low, size in spans(width - edge, 2 * LANES)]
    late_down = [(1, part * local // 2, local // 2) for part in range(4)]
    *rest, done = fetch((up_weight, down_weight), late + late_down, (mine,))
    feed, middle = feed_half(
        own_blocks,
        mine,
        theirs,
        paired,
        mod,
        ups + rest[: len(late)],
        rest[len(late) :],
        down_weight,
    )
    if paired:
        fed_there = flipped(feed[tile_rows:], "row", 1, n_row)
    else:
        feed = lax.psum_scatter(feed.astype(jnp.float32), "row", scatter_dimension=0, tiled=True)
        fed_there = feed
        middle = lax.dynamic_slice_in_dim(
            middle, lax.axis_index("row") * tile_rows, tile_rows, 0
        )
    leaving, raw_velocity = final_step(middle, feed, fed_there, paired, mod, final_weight.T)
    raw_velocity = raw_velocity.reshape(latent.shape)
    partner = flipped(raw_velocity, "item", 1, lax.axis_size("item"))
    is_guided = lax.axis_index("item") % 2 == 0
    guided = jnp.where(is_guided, raw_velocity, partner)
    unguided = jnp.where(is_guided, partner, raw_velocity)
    velocity = unguided + GUIDANCE * (guided - unguided)
    position = step_index[0].astype(jnp.float32)
    step_size = noise_level(position + 1.0) - noise_level(position)
    return (leaving.reshape(tokens.shape), velocity, latent + step_size * velocity)


def solution(mesh):
    in_specs = (
        P("item", "row", "col", None),
        P("item", None, None, "row"),
        P("item"),
        P("item", None, None),
        P(None, None, "row"),
        P(),
        P("row", None),
        P(None, "row"),
        P("row", None),
        P(),
        P(),
        P("item", "row", "col"),
    )
    out_specs = (P("item", "row", "col", None), P("item", "row", "col"), P("item", "row", "col"))
    return jax.shard_map(
        on_device, mesh=mesh, in_specs=in_specs, out_specs=out_specs, check_vma=False
    )
```

```python
import functools

import jax
import jax.numpy as jnp
from jax import lax
from jax.experimental import pallas as pl
from jax.experimental.pallas import tpu as pltpu
from jax.sharding import PartitionSpec as P

HD = 64
STEPS = 28

EPSILON = 1e-06
SHIFT_FACTOR = 3.0
GUIDANCE = 4.5
MASKED = -1e30

LANES = 128
TILE = 256
ROWS = 16
SCOPED = 16 << 20
SCOPED_FETCH = 17 << 20
EARLY = 1

IN_VMEM = pl.BlockSpec(memory_space=pltpu.VMEM)
IN_PLACE = pl.BlockSpec(memory_space=pl.ANY)


def noise_level(position):
    linear = 1.0 - position / STEPS
    return SHIFT_FACTOR * linear / (1.0 + (SHIFT_FACTOR - 1.0) * linear)


def layer_norm(values):
    center = values - jnp.mean(values, axis=-1, keepdims=True)
    spread = jnp.mean(center * center, axis=-1, keepdims=True)
    return center * lax.rsqrt(spread + EPSILON)


def modulated(values, mod_ref, shift_row, scale_row):
    scale = 1.0 + mod_ref[scale_row : scale_row + 1, :]
    shift = mod_ref[shift_row : shift_row + 1, :]
    return (layer_norm(values) * scale + shift).astype(jnp.bfloat16)


def spans(width, step):
    return [(low, min(step, width - low)) for low in range(0, width, step)]


def for_rows(rows, step, body):
    if rows <= 2 * LANES:
        for low in range(0, rows, step):
            body(low)
    else:
        pl.loop(0, rows // step)(lambda at: body(pl.multiple_of(at * step, step)))


def in_hbm(array):
    return pltpu.with_memory_space_constraint(array, pltpu.HBM)


def in_vmem(array):
    return pltpu.with_memory_space_constraint(array, pltpu.VMEM)


def bytes_of(arrays):
    return sum(a.size * a.dtype.itemsize for a in arrays)


def copies_of(parts, sources, targets, sems, shares):
    share = lax.axis_index("col") % shares
    copies = []
    for index, ((at, low, rows, width), target) in enumerate(zip(parts, targets)):
        source = sources[at]
        if source.shape[1] == width:
            first = low + share * (source.shape[0] // shares)
            piece = source.at[pl.ds(pl.multiple_of(first, ROWS), rows)]
        else:
            piece = source.at[pl.ds(low, rows), pl.ds(pl.multiple_of(share * width, LANES), width)]
        copies.append(pltpu.make_async_copy(piece, target, sems.at[index]))
    return copies


def fetch_kernel(parts, shares, n_sources, n_after, *refs):
    sources, refs = refs[:n_sources], refs[n_sources + n_after :]
    targets, done, sems = refs[: len(parts)], refs[-2], refs[-1]
    copies = copies_of(parts, sources, targets, sems, shares)
    for copy in copies:
        copy.start()
    done[...] = jnp.zeros_like(done)
    for copy in copies:
        copy.wait()


def first_kernel(parts, text_hbm, source, *refs):
    *targets, split, text, text_sem, sems = refs
    text_copy = pltpu.make_async_copy(text_hbm, text, text_sem)
    text_copy.start()
    copies = copies_of(parts, (source,), targets, sems, 1)
    for copy in copies:
        copy.start()
    count = text.shape[0]
    split[...] = jnp.zeros_like(split)
    text_copy.wait()
    split[0, :count, :] = text[:, 0, :]
    split[1, :count, :] = text[:, 1, :]
    for copy in copies:
        copy.wait()


def first_step(text, source, parts):
    rows = -(-text.shape[0] // ROWS) * ROWS
    moved = sum(2 * size * width for at, low, size, width in parts)
    return pl.pallas_call(
        functools.partial(first_kernel, parts),
        out_shape=[pltpu.VMEM((size, width), jnp.bfloat16) for at, low, size, width in parts]
        + [jax.ShapeDtypeStruct((2, rows, text.shape[2]), jnp.bfloat16)],
        in_specs=[IN_PLACE] * 2,
        out_specs=[IN_VMEM] * (len(parts) + 1),
        scratch_shapes=[
            pltpu.VMEM(text.shape, jnp.bfloat16),
            pltpu.SemaphoreType.DMA,
            pltpu.SemaphoreType.DMA((len(parts),)),
        ],
        compiler_params=pltpu.CompilerParams(vmem_limit_bytes=SCOPED_FETCH),
        cost_estimate=pl.CostEstimate(flops=0, bytes_accessed=2 * moved, transcendentals=0),
    )(in_hbm(text), in_hbm(source))


def fetch(sources, parts, after=(), shares=1):
    shapes = [(rows, width) for at, low, rows, width in parts]
    moved = sum(2 * rows * width for rows, width in shapes)
    return pl.pallas_call(
        functools.partial(fetch_kernel, parts, shares, len(sources), len(after)),
        out_shape=[pltpu.VMEM(shape, jnp.bfloat16) for shape in shapes]
        + [jax.ShapeDtypeStruct((8, LANES), jnp.float32)],
        in_specs=[IN_PLACE] * (len(sources) + len(after)),
        out_specs=[IN_VMEM] * (len(parts) + 1),
        scratch_shapes=[pltpu.SemaphoreType.DMA((len(parts),))],
        compiler_params=pltpu.CompilerParams(vmem_limit_bytes=SCOPED_FETCH),
        cost_estimate=pl.CostEstimate(flops=0, bytes_accessed=2 * moved, transcendentals=0),
    )(*[in_hbm(source) for source in sources], *after)


def norm_kernel(n_blocks, *refs):
    blocks, mod, normed = refs[:n_blocks], refs[n_blocks], refs[-1]
    for at, block in enumerate(blocks):
        rows = block.shape[0]
        values = block[...].astype(jnp.float32)
        normed[at * rows : (at + 1) * rows, :] = modulated(values, mod, 0, 1)


def norm_step(blocks, mod):
    rows, width = sum(block.shape[0] for block in blocks), mod.shape[1]
    return pl.pallas_call(
        functools.partial(norm_kernel, len(blocks)),
        out_shape=jax.ShapeDtypeStruct((rows, width), jnp.bfloat16),
        in_specs=[IN_VMEM] * (len(blocks) + 1),
        out_specs=IN_VMEM,
        compiler_params=pltpu.CompilerParams(vmem_limit_bytes=SCOPED_FETCH),
        cost_estimate=pl.CostEstimate(
            flops=10 * rows * width, bytes_accessed=4 * rows * width, transcendentals=0
        ),
    )(*blocks, mod)


def attention_kernel(n_normed, n_blocks, own_rows, *refs):
    ready, refs = refs[:n_normed], refs[n_normed:]
    blocks = refs[:n_blocks]
    length, mod, gains, text, *in_ws, out_w = refs[n_blocks : n_blocks + 8]
    out, normed, q_ref, k_ref, v_ref, att_ref = refs[-6:]

    all_rows, width = normed.shape
    local = in_ws[0].shape[1]
    low = 0
    for part in ready:
        normed[low : low + part.shape[0], :] = part[...]
        low += part.shape[0]
    for block in blocks:

        def norm_rows(at, block=block, low=low):
            values = block[pl.ds(at, ROWS), :].astype(jnp.float32)
            normed[pl.ds(low + at, ROWS), :] = modulated(values, mod, 0, 1)

        for_rows(block.shape[0], ROWS, norm_rows)
        low += block.shape[0]

    tile = min(TILE, local)
    head_of_row = lax.broadcasted_iota(jnp.int32, (tile, tile), 0) // HD
    head_of_col = lax.broadcasted_iota(jnp.int32, (tile, tile), 1) // HD
    gain = jnp.concatenate([gains[...]] * (tile // HD), axis=1)
    same_head = (head_of_row == head_of_col).astype(jnp.bfloat16)

    def head_norm(values, gain_row):
        squares = values * values
        high = squares.astype(jnp.bfloat16)
        rest = (squares - high.astype(jnp.float32)).astype(jnp.bfloat16)
        total = jnp.dot(high, same_head, preferred_element_type=jnp.float32)
        total += jnp.dot(rest, same_head, preferred_element_type=jnp.float32)
        return values * lax.rsqrt(total * (1.0 / HD) + EPSILON) * gain_row

    for at, size in spans(local, tile):
        cols = slice(at, at + size)

        def project(first, rows, part):
            return jnp.dot(
                normed[pl.ds(first, rows), :],
                in_ws[part][:, cols],
                preferred_element_type=jnp.float32,
            )

        def keys_values(first):
            rows = min(LANES, all_rows)
            k_ref[pl.ds(first, rows), cols] = head_norm(
                project(first, rows, 1), gain[1:2, :size]
            ).astype(jnp.bfloat16)
            v_ref[pl.ds(first, rows), cols] = project(first, rows, 2).astype(jnp.bfloat16)

        def queries(first):
            rows = min(LANES, own_rows)
            q_ref[pl.ds(first, rows), cols] = head_norm(
                project(first, rows, 0), gain[0:1, :size]
            ).astype(jnp.bfloat16)

        for_rows(own_rows, min(LANES, own_rows), queries)
        for_rows(all_rows, min(LANES, all_rows), keys_values)

    used = lax.broadcasted_iota(jnp.int32, (1, text.shape[1]), 1) < length[...]
    first_head = lax.broadcasted_iota(jnp.int32, (1, LANES), 1) < HD
    contract = (((1,), (1,)), ((), ()))
    for at, size in spans(local, LANES):
        cols = slice(at, at + size)
        q = q_ref[:, cols]
        zero = jnp.zeros_like(q)
        pair = jnp.concatenate([jnp.where(first_head, q, zero), jnp.where(first_head, zero, q)], 0)
        scores = HD ** (-0.5) * lax.dot_general(
            pair, k_ref[:, cols], contract, preferred_element_type=jnp.float32
        )
        text_scores = HD ** (-0.5) * lax.dot_general(
            pair, text[0, :, cols], contract, preferred_element_type=jnp.float32
        )
        text_scores = jnp.where(used, text_scores, MASKED)
        largest = jnp.maximum(
            jnp.max(scores, axis=-1, keepdims=True), jnp.max(text_scores, axis=-1, keepdims=True)
        )
        weights = jnp.exp(scores - largest)
        text_weights = jnp.exp(text_scores - largest)
        total = jnp.sum(weights, axis=-1, keepdims=True)
        total += jnp.sum(text_weights, axis=-1, keepdims=True)
        mixed = jnp.dot(
            weights.astype(jnp.bfloat16), v_ref[:, cols], preferred_element_type=jnp.float32
        )
        mixed += jnp.dot(
            text_weights.astype(jnp.bfloat16), text[1, :, cols], preferred_element_type=jnp.float32
        )
        mixed = mixed / total
        att_ref[:, cols] = jnp.where(first_head, mixed[:own_rows], mixed[own_rows:]).astype(
            jnp.bfloat16
        )

    for at, size in spans(width, TILE):
        cols = slice(at, at + size)
        out[:, cols] = jnp.dot(
            att_ref[...], out_w[:, cols], preferred_element_type=jnp.float32
        ).astype(jnp.bfloat16)


def attention_half(ready, blocks, own_rows, length, mod, gains, text, in_ws, out_w, after):
    width, local = mod.shape[1], out_w.shape[0]
    all_rows = sum(part.shape[0] for part in (*ready, *blocks))
    scoped = SCOPED_FETCH if all_rows <= LANES else 48 << 20
    return pl.pallas_call(
        functools.partial(attention_kernel, len(ready), len(blocks), own_rows),
        out_shape=jax.ShapeDtypeStruct((own_rows, width), jnp.bfloat16),
        in_specs=[IN_VMEM] * (len(ready) + len(blocks)) + [IN_VMEM] * 8 + [IN_PLACE],
        out_specs=IN_VMEM,
        scratch_shapes=[
            pltpu.VMEM((all_rows, width), jnp.bfloat16),
            pltpu.VMEM((own_rows, local), jnp.bfloat16),
            pltpu.VMEM((all_rows, local), jnp.bfloat16),
            pltpu.VMEM((all_rows, local), jnp.bfloat16),
            pltpu.VMEM((own_rows, local), jnp.bfloat16),
        ],
        compiler_params=pltpu.CompilerParams(vmem_limit_bytes=scoped),
    )(
        *ready,
        *blocks,
        length,
        mod,
        gains,
        text,
        *[in_vmem(part) for part in in_ws],
        in_vmem(out_w),
        after,
    )


def middle_kernel(n_blocks, paired, *refs):
    blocks = refs[:n_blocks]
    mine, theirs, mod, after, fed, middle = refs[n_blocks:]
    rows = fed.shape[0]
    tile = rows // n_blocks
    step = tile if tile <= LANES else ROWS
    for at, block in enumerate(blocks):

        def norm_rows(low, at=at, block=block):
            here = pl.ds(at * tile + low, step)
            attention = mine[here, :].astype(jnp.float32)
            if paired:
                there = pl.ds((at * tile + low + rows // 2) % rows, step)
                attention += theirs[there, :].astype(jnp.float32)
            values = block[pl.ds(low, step), :].astype(jnp.float32) + mod[2:3, :] * attention
            middle[here, :] = values
            fed[here, :] = modulated(values, mod, 3, 4)

        for_rows(tile, step, norm_rows)


def middle_step(blocks, mine, theirs, paired, mod, after):
    rows, width = mine.shape
    return pl.pallas_call(
        functools.partial(middle_kernel, len(blocks), paired),
        out_shape=[
            jax.ShapeDtypeStruct((rows, width), jnp.bfloat16),
            jax.ShapeDtypeStruct((rows, width), jnp.float32),
        ],
        in_specs=[IN_VMEM] * (len(blocks) + 3) + [IN_PLACE],
        out_specs=[IN_VMEM] * 2,
        compiler_params=pltpu.CompilerParams(vmem_limit_bytes=SCOPED),
    )(*blocks, mine, theirs, mod, after)


def feed_kernel(n_fed, n_ups, n_downs, n_outs, *refs):
    feds, refs = refs[:n_fed], refs[n_fed:]
    ups, refs = refs[:n_ups], refs[n_ups:]
    downs, outs = refs[:n_downs], refs[n_downs : n_downs + n_outs]
    fed, hidden = refs[-2:]
    rows, width = fed.shape
    units = hidden.shape[1]
    for at, part in enumerate(feds):
        fed[at * part.shape[0] : (at + 1) * part.shape[0], :] = part[...]

    def product(left, parts, cols):
        sums, low = 0.0, 0
        for part in parts:
            here = slice(low, low + part.shape[0])
            sums += jnp.dot(left[:, here], part[:, cols], preferred_element_type=jnp.float32)
            low = here.stop
        return sums

    for at, size in spans(units, TILE):
        cols = slice(at, at + size)
        hidden[:, cols] = jax.nn.gelu(product(fed, ups, cols), approximate=True).astype(jnp.bfloat16)

    each = rows // n_outs
    for at, size in spans(width, TILE):
        cols = slice(at, at + size)
        sums = product(hidden, downs, cols).astype(jnp.bfloat16)
        for index, out in enumerate(outs):
            out[:, cols] = sums[index * each : (index + 1) * each]


def feed_half(feds, ups, downs, n_outs):
    rows = sum(fed.shape[0] for fed in feds)
    width, units = downs[0].shape[1], ups[0].shape[1]
    scoped = SCOPED if rows <= LANES else 32 << 20
    return pl.pallas_call(
        functools.partial(feed_kernel, len(feds), len(ups), len(downs), n_outs),
        out_shape=[jax.ShapeDtypeStruct((rows // n_outs, width), jnp.bfloat16)] * n_outs,
        in_specs=[IN_VMEM] * (len(feds) + len(ups) + len(downs)),
        out_specs=[IN_VMEM] * n_outs,
        scratch_shapes=[
            pltpu.VMEM((rows, width), jnp.bfloat16),
            pltpu.VMEM((rows, units), jnp.bfloat16),
        ],
        compiler_params=pltpu.CompilerParams(vmem_limit_bytes=scoped),
    )(*feds, *[in_vmem(part) for part in (*ups, *downs)])


def final_kernel(n_feeds, middle, *refs):
    feeds = refs[:n_feeds]
    mod, final_w, leaving_out, velocity = refs[n_feeds:]
    feed = feeds[0][...].astype(jnp.float32)
    for other in feeds[1:]:
        feed += other[...].astype(jnp.float32)
    leaving = middle[: feed.shape[0], :] + mod[5:6, :] * feed
    leaving_out[...] = leaving.astype(jnp.bfloat16)
    raw = lax.dot_general(
        modulated(leaving, mod, 6, 7),
        final_w[...],
        (((1,), (1,)), ((), ())),
        preferred_element_type=jnp.float32,
    )
    velocity[...] = jnp.concatenate([raw[at : at + 1, :] for at in range(raw.shape[0])], axis=1)


def final_step(middle, feeds, mod, final_w):
    rows, width = feeds[0].shape
    return pl.pallas_call(
        functools.partial(final_kernel, len(feeds)),
        out_shape=[
            jax.ShapeDtypeStruct((rows, width), jnp.bfloat16),
            jax.ShapeDtypeStruct((1, rows * final_w.shape[0]), jnp.float32),
        ],
        in_specs=[IN_VMEM] * (3 + len(feeds)),
        out_specs=[IN_VMEM] * 2,
        compiler_params=pltpu.CompilerParams(vmem_limit_bytes=SCOPED),
    )(middle, *feeds, mod, final_w)


def guided_kernel(raw, partner, latent, index, velocity, latent_next):
    position = index[...].astype(jnp.float32)
    step_size = noise_level(position + 1.0) - noise_level(position)
    is_guided = lax.axis_index("item") % 2 == 0
    guided = jnp.where(is_guided, raw[...], partner[...])
    unguided = jnp.where(is_guided, partner[...], raw[...])
    combined = unguided + GUIDANCE * (guided - unguided)
    velocity[...] = combined
    latent_next[...] = latent[...] + step_size * combined


def guided_step(raw, partner, latent, index):
    return pl.pallas_call(
        guided_kernel,
        out_shape=[jax.ShapeDtypeStruct(raw.shape, jnp.float32)] * 2,
        in_specs=[IN_VMEM] * 4,
        out_specs=[IN_VMEM] * 2,
        compiler_params=pltpu.CompilerParams(vmem_limit_bytes=SCOPED),
    )(raw, partner, latent, index)


def flipped(value, axes, mask, count):
    return lax.ppermute(value, axes, [(source, source ^ mask) for source in range(count)])


def on_device(
    tokens,
    text_keys_values,
    text_length,
    modulation,
    input_weight,
    norm_gain,
    output_weight,
    up_weight,
    down_weight,
    final_weight,
    step_index,
    latent,
):
    n_row, n_col = lax.axis_size("row"), lax.axis_size("col")
    width = tokens.shape[3]
    tile = tokens.reshape(-1, width)
    local = input_weight.shape[2]
    mod = modulation[0]
    in_w = input_weight.transpose(1, 0, 2).reshape(3 * width, local)
    paired = n_row == 2
    both = ("row", "col")
    count = n_row * n_col
    tile_rows = tile.shape[0]
    own_rows = n_row * tile_rows

    split = paired and n_col == 4
    shares = 2 if split else 1
    units = down_weight.shape[0] // shares
    up_parts = [(0, low, size, units) for low, size in spans(width, 3 * TILE)]
    thirds = [(0, part * width, width, local) for part in range(3)]
    step = max(LANES, units // 4 // TILE * TILE)
    down_parts = [(0, low, size, width) for low, size in spans(units, step)]
    if split:
        near = [tile] + [flipped(tile, both, mask, count) for mask in (n_col, 2, n_col + 2)]
        *in_ws, text = first_step(text_keys_values[0], in_w, thirds)
        *near, text = lax.optimization_barrier((*near, text))
        own_blocks = near[:2]
        normed = norm_step(near, mod)
        ready, far = [normed, flipped(normed, both, 1, count)], []
    else:
        gathered = lax.all_gather(tile, ("col", "row"), axis=0, tiled=True)
        far = [jnp.roll(gathered, -lax.axis_index("col") * own_rows, axis=0)]
        own_blocks = [far[0][:own_rows]]
        ready, normed = [], tile
        *in_ws, text = first_step(text_keys_values[0], in_w, thirds)
    *early, done = fetch((down_weight,), down_parts[:EARLY], (normed,), shares)
    mine = attention_half(
        ready,
        far,
        own_rows,
        text_length.reshape(1, 1),
        mod,
        norm_gain,
        text,
        in_ws,
        output_weight,
        done,
    )
    if paired:
        theirs = flipped(mine, "row", 1, n_row)
    else:
        mine = lax.psum(mine.astype(jnp.float32), "row")
        theirs = mine
    *ups, done = fetch((up_weight,), up_parts, (mine,), shares)
    fed, middle = middle_step(own_blocks, mine, theirs, paired, mod, done)
    *late, done = fetch((down_weight,), down_parts[EARLY:], (fed,), shares)
    downs = early + late
    if split:
        feds = [fed, flipped(fed, both, 1, count)]
        feed, *others = feed_half(feds, ups, downs, 4)
        feeds = [feed] + [
            flipped(part, both, mask, count) for part, mask in zip(others, (n_col, 1, n_col + 1))
        ]
    else:
        (feed,) = feed_half([fed], ups, downs, 1)
        if paired:
            feeds = [feed[:tile_rows], flipped(feed[tile_rows:], "row", 1, n_row)]
        else:
            feeds = [
                lax.psum_scatter(feed.astype(jnp.float32), "row", scatter_dimension=0, tiled=True)
            ]
            middle = lax.dynamic_slice_in_dim(
                middle, lax.axis_index("row") * tile_rows, tile_rows, 0
            )
    leaving, raw_velocity = final_step(middle, feeds, mod, final_weight.T)
    partner = flipped(raw_velocity, "item", 1, lax.axis_size("item"))
    velocity, latent_next = guided_step(
        raw_velocity, partner, latent.reshape(raw_velocity.shape), step_index.reshape(1, 1)
    )
    return (
        leaving.reshape(tokens.shape),
        velocity.reshape(latent.shape),
        latent_next.reshape(latent.shape),
    )


def solution(mesh):
    in_specs = (
        P("item", "row", "col", None),
        P("item", None, None, "row"),
        P("item"),
        P("item", None, None),
        P(None, None, "row"),
        P(),
        P("row", None),
        P(None, "row"),
        P("row", None),
        P(),
        P(),
        P("item", "row", "col"),
    )
    out_specs = (P("item", "row", "col", None), P("item", "row", "col"), P("item", "row", "col"))
    return jax.shard_map(
        on_device, mesh=mesh, in_specs=in_specs, out_specs=out_specs, check_vma=False
    )
```

```python
import functools

import jax
import jax.numpy as jnp
from jax import lax
from jax.experimental import pallas as pl
from jax.experimental.pallas import tpu as pltpu
from jax.sharding import PartitionSpec as P

HD = 64
STEPS = 28

EPSILON = 1e-06
SHIFT_FACTOR = 3.0
GUIDANCE = 4.5
MASKED = -1e30

LANES = 128
TILE = 256
ROWS = 16
SCOPED = 16 << 20
SCOPED_FETCH = 17 << 20

IN_VMEM = pl.BlockSpec(memory_space=pltpu.VMEM)
IN_PLACE = pl.BlockSpec(memory_space=pl.ANY)


def noise_level(position):
    linear = 1.0 - position / STEPS
    return SHIFT_FACTOR * linear / (1.0 + (SHIFT_FACTOR - 1.0) * linear)


def layer_norm(values):
    center = values - jnp.mean(values, axis=-1, keepdims=True)
    spread = jnp.mean(center * center, axis=-1, keepdims=True)
    return center * lax.rsqrt(spread + EPSILON)


def modulated(values, mod_ref, shift_row, scale_row):
    scale = 1.0 + mod_ref[scale_row : scale_row + 1, :]
    shift = mod_ref[shift_row : shift_row + 1, :]
    return (layer_norm(values) * scale + shift).astype(jnp.bfloat16)


def spans(width, step):
    return [(low, min(step, width - low)) for low in range(0, width, step)]


def for_rows(rows, step, body):
    if rows <= 2 * LANES:
        for low in range(0, rows, step):
            body(low)
    else:
        pl.loop(0, rows // step)(lambda at: body(pl.multiple_of(at * step, step)))


def in_hbm(array):
    return pltpu.with_memory_space_constraint(array, pltpu.HBM)


def in_vmem(array):
    return pltpu.with_memory_space_constraint(array, pltpu.VMEM)


def bytes_of(arrays):
    return sum(a.size * a.dtype.itemsize for a in arrays)


def copies_of(parts, sources, targets, sems, shares):
    share = lax.axis_index("col") % shares
    copies = []
    for index, ((at, low, rows, width), target) in enumerate(zip(parts, targets)):
        source = sources[at]
        if source.shape[1] == width:
            first = low + share * (source.shape[0] // shares)
            piece = source.at[pl.ds(pl.multiple_of(first, ROWS), rows)]
        else:
            piece = source.at[pl.ds(low, rows), pl.ds(pl.multiple_of(share * width, LANES), width)]
        copies.append(pltpu.make_async_copy(piece, target, sems.at[index]))
    return copies


def fetch_kernel(parts, shares, n_sources, n_after, *refs):
    sources, refs = refs[:n_sources], refs[n_sources + n_after :]
    targets, done, sems = refs[: len(parts)], refs[-2], refs[-1]
    copies = copies_of(parts, sources, targets, sems, shares)
    for copy in copies:
        copy.start()
    done[...] = jnp.zeros_like(done)
    for copy in copies:
        copy.wait()


def first_kernel(parts, text_hbm, source, *refs):
    *targets, split, text, text_sem, sems = refs
    text_copy = pltpu.make_async_copy(text_hbm, text, text_sem)
    text_copy.start()
    copies = copies_of(parts, (source,), targets, sems, 1)
    for copy in copies:
        copy.start()
    count = text.shape[0]
    split[...] = jnp.zeros_like(split)
    text_copy.wait()
    split[0, :count, :] = text[:, 0, :]
    split[1, :count, :] = text[:, 1, :]
    for copy in copies:
        copy.wait()


def first_step(text, source, parts):
    rows = -(-text.shape[0] // ROWS) * ROWS
    moved = sum(2 * size * width for at, low, size, width in parts)
    return pl.pallas_call(
        functools.partial(first_kernel, parts),
        out_shape=[pltpu.VMEM((size, width), jnp.bfloat16) for at, low, size, width in parts]
        + [jax.ShapeDtypeStruct((2, rows, text.shape[2]), jnp.bfloat16)],
        in_specs=[IN_PLACE] * 2,
        out_specs=[IN_VMEM] * (len(parts) + 1),
        scratch_shapes=[
            pltpu.VMEM(text.shape, jnp.bfloat16),
            pltpu.SemaphoreType.DMA,
            pltpu.SemaphoreType.DMA((len(parts),)),
        ],
        compiler_params=pltpu.CompilerParams(vmem_limit_bytes=SCOPED_FETCH),
        cost_estimate=pl.CostEstimate(flops=0, bytes_accessed=2 * moved, transcendentals=0),
    )(in_hbm(text), in_hbm(source))


def fetch(sources, parts, after=(), shares=1):
    shapes = [(rows, width) for at, low, rows, width in parts]
    moved = sum(2 * rows * width for rows, width in shapes)
    return pl.pallas_call(
        functools.partial(fetch_kernel, parts, shares, len(sources), len(after)),
        out_shape=[pltpu.VMEM(shape, jnp.bfloat16) for shape in shapes]
        + [jax.ShapeDtypeStruct((8, LANES), jnp.float32)],
        in_specs=[IN_PLACE] * (len(sources) + len(after)),
        out_specs=[IN_VMEM] * (len(parts) + 1),
        scratch_shapes=[pltpu.SemaphoreType.DMA((len(parts),))],
        compiler_params=pltpu.CompilerParams(vmem_limit_bytes=SCOPED_FETCH),
        cost_estimate=pl.CostEstimate(flops=0, bytes_accessed=2 * moved, transcendentals=0),
    )(*[in_hbm(source) for source in sources], *after)


def norm_kernel(n_blocks, *refs):
    blocks, mod, normed = refs[:n_blocks], refs[n_blocks], refs[-1]
    for at, block in enumerate(blocks):
        rows = block.shape[0]
        values = block[...].astype(jnp.float32)
        normed[at * rows : (at + 1) * rows, :] = modulated(values, mod, 0, 1)


def norm_step(blocks, mod):
    rows, width = sum(block.shape[0] for block in blocks), mod.shape[1]
    return pl.pallas_call(
        functools.partial(norm_kernel, len(blocks)),
        out_shape=jax.ShapeDtypeStruct((rows, width), jnp.bfloat16),
        in_specs=[IN_VMEM] * (len(blocks) + 1),
        out_specs=IN_VMEM,
        compiler_params=pltpu.CompilerParams(vmem_limit_bytes=SCOPED_FETCH),
        cost_estimate=pl.CostEstimate(
            flops=10 * rows * width, bytes_accessed=4 * rows * width, transcendentals=0
        ),
    )(*blocks, mod)


def attention_kernel(n_normed, n_blocks, own_rows, *refs):
    ready, refs = refs[:n_normed], refs[n_normed:]
    blocks = refs[:n_blocks]
    length, mod, gains, text, *in_ws, out_w = refs[n_blocks : n_blocks + 8]
    out, normed, q_ref, k_ref, v_ref, att_ref = refs[-6:]

    all_rows, width = normed.shape
    local = in_ws[0].shape[1]
    low = 0
    for part in ready:
        normed[low : low + part.shape[0], :] = part[...]
        low += part.shape[0]
    for block in blocks:

        def norm_rows(at, block=block, low=low):
            values = block[pl.ds(at, ROWS), :].astype(jnp.float32)
            normed[pl.ds(low + at, ROWS), :] = modulated(values, mod, 0, 1)

        for_rows(block.shape[0], ROWS, norm_rows)
        low += block.shape[0]

    tile = min(TILE, local)
    head_of_row = lax.broadcasted_iota(jnp.int32, (tile, tile), 0) // HD
    head_of_col = lax.broadcasted_iota(jnp.int32, (tile, tile), 1) // HD
    gain = jnp.concatenate([gains[...]] * (tile // HD), axis=1)
    same_head = (head_of_row == head_of_col).astype(jnp.bfloat16)

    def head_norm(values, gain_rows):
        squares = (values * values).astype(jnp.bfloat16)
        total = jnp.dot(squares, same_head, preferred_element_type=jnp.float32)
        return (values * lax.rsqrt(total * (1.0 / HD) + EPSILON) * gain_rows).astype(jnp.bfloat16)

    def project(first, rows, part, cols):
        return jnp.dot(
            normed[pl.ds(first, rows), :], in_ws[part][:, cols], preferred_element_type=jnp.float32
        )

    def project_rows(first, rows, part, target, columns):
        raws = [project(first, rows, part, cols) for cols in columns]
        normals = [head_norm(raw, gain[part : part + 1, :]) for raw in raws]
        for cols, normal in zip(columns, normals):
            target[pl.ds(first, rows), cols] = normal

    columns = [slice(at, at + size) for at, size in spans(local, tile)]
    own_step, all_step = min(LANES, own_rows), min(LANES, all_rows)

    def keys_values(first):
        project_rows(first, all_step, 1, k_ref, columns)
        for cols in columns:
            values = project(first, all_step, 2, cols)
            v_ref[pl.ds(first, all_step), cols] = values.astype(jnp.bfloat16)

    for_rows(own_rows, own_step, lambda first: project_rows(first, own_step, 0, q_ref, columns))
    for_rows(all_rows, all_step, keys_values)

    used = lax.broadcasted_iota(jnp.int32, (1, text.shape[1]), 1) < length[...]
    first_head = lax.broadcasted_iota(jnp.int32, (1, LANES), 1) < HD
    contract = (((1,), (1,)), ((), ()))
    def attend(group):
        scores = []
        for cols in group:
            q = q_ref[:, cols]
            zero = jnp.zeros_like(q)
            pair = jnp.concatenate(
                [jnp.where(first_head, q, zero), jnp.where(first_head, zero, q)], 0
            )
            image = lax.dot_general(
                pair, k_ref[:, cols], contract, preferred_element_type=jnp.float32
            )
            other = lax.dot_general(
                pair, text[0, :, cols], contract, preferred_element_type=jnp.float32
            )
            scores.append(
                (HD ** (-0.5) * image, jnp.where(used, HD ** (-0.5) * other, MASKED))
            )
        largest = [
            jnp.maximum(
                jnp.max(image, axis=-1, keepdims=True), jnp.max(other, axis=-1, keepdims=True)
            )
            for image, other in scores
        ]
        weights = [
            (jnp.exp(image - top), jnp.exp(other - top))
            for (image, other), top in zip(scores, largest)
        ]
        totals = [
            jnp.sum(image, axis=-1, keepdims=True) + jnp.sum(other, axis=-1, keepdims=True)
            for image, other in weights
        ]
        for cols, (image, other), total in zip(group, weights, totals):
            mixed = jnp.dot(
                image.astype(jnp.bfloat16), v_ref[:, cols], preferred_element_type=jnp.float32
            )
            mixed += jnp.dot(
                other.astype(jnp.bfloat16), text[1, :, cols], preferred_element_type=jnp.float32
            )
            mixed = mixed / total
            att_ref[:, cols] = jnp.where(first_head, mixed[:own_rows], mixed[own_rows:]).astype(
                jnp.bfloat16
            )

    pairs = [slice(at, at + size) for at, size in spans(local, LANES)]
    group = len(pairs) if all_rows <= LANES else 1
    for first in range(0, len(pairs), group):
        attend(pairs[first : first + group])

    for at, size in spans(width, TILE):
        cols = slice(at, at + size)
        out[:, cols] = jnp.dot(
            att_ref[...], out_w[:, cols], preferred_element_type=jnp.float32
        ).astype(jnp.bfloat16)


def attention_half(ready, blocks, own_rows, length, mod, gains, text, in_ws, out_w, after):
    width, local = mod.shape[1], out_w.shape[0]
    all_rows = sum(part.shape[0] for part in (*ready, *blocks))
    scoped = SCOPED_FETCH if all_rows <= LANES else 48 << 20
    return pl.pallas_call(
        functools.partial(attention_kernel, len(ready), len(blocks), own_rows),
        out_shape=jax.ShapeDtypeStruct((own_rows, width), jnp.bfloat16),
        in_specs=[IN_VMEM] * (len(ready) + len(blocks)) + [IN_VMEM] * 8 + [IN_PLACE],
        out_specs=IN_VMEM,
        scratch_shapes=[
            pltpu.VMEM((all_rows, width), jnp.bfloat16),
            pltpu.VMEM((own_rows, local), jnp.bfloat16),
            pltpu.VMEM((all_rows, local), jnp.bfloat16),
            pltpu.VMEM((all_rows, local), jnp.bfloat16),
            pltpu.VMEM((own_rows, local), jnp.bfloat16),
        ],
        compiler_params=pltpu.CompilerParams(vmem_limit_bytes=scoped),
    )(
        *ready,
        *blocks,
        length,
        mod,
        gains,
        text,
        *[in_vmem(part) for part in in_ws],
        in_vmem(out_w),
        after,
    )


def middle_kernel(n_blocks, paired, *refs):
    blocks = refs[:n_blocks]
    mine, theirs, mod, after, fed, middle = refs[n_blocks:]
    rows = fed.shape[0]
    tile = rows // n_blocks
    step = tile if tile <= LANES else ROWS
    for at, block in enumerate(blocks):

        def norm_rows(low, at=at, block=block):
            here = pl.ds(at * tile + low, step)
            attention = mine[here, :].astype(jnp.float32)
            if paired:
                there = pl.ds((at * tile + low + rows // 2) % rows, step)
                attention += theirs[there, :].astype(jnp.float32)
            values = block[pl.ds(low, step), :].astype(jnp.float32) + mod[2:3, :] * attention
            middle[here, :] = values
            fed[here, :] = modulated(values, mod, 3, 4)

        for_rows(tile, step, norm_rows)


def middle_step(blocks, mine, theirs, paired, mod, after):
    rows, width = mine.shape
    return pl.pallas_call(
        functools.partial(middle_kernel, len(blocks), paired),
        out_shape=[
            jax.ShapeDtypeStruct((rows, width), jnp.bfloat16),
            jax.ShapeDtypeStruct((rows, width), jnp.float32),
        ],
        in_specs=[IN_VMEM] * (len(blocks) + 3) + [IN_PLACE],
        out_specs=[IN_VMEM] * 2,
        compiler_params=pltpu.CompilerParams(vmem_limit_bytes=SCOPED),
    )(*blocks, mine, theirs, mod, after)


def feed_kernel(n_fed, n_ups, n_downs, n_outs, *refs):
    feds, refs = refs[:n_fed], refs[n_fed:]
    ups, refs = refs[:n_ups], refs[n_ups:]
    downs, outs = refs[:n_downs], refs[n_downs : n_downs + n_outs]
    fed, hidden = refs[-2:]
    rows, width = fed.shape
    units = hidden.shape[1]
    for at, part in enumerate(feds):
        fed[at * part.shape[0] : (at + 1) * part.shape[0], :] = part[...]

    def product(left, parts, cols):
        sums, low = 0.0, 0
        for part in parts:
            here = slice(low, low + part.shape[0])
            sums += jnp.dot(left[:, here], part[:, cols], preferred_element_type=jnp.float32)
            low = here.stop
        return sums

    for at, size in spans(units, TILE):
        cols = slice(at, at + size)
        hidden[:, cols] = jax.nn.gelu(product(fed, ups, cols), approximate=True).astype(jnp.bfloat16)

    each = rows // n_outs
    for at, size in spans(width, TILE):
        cols = slice(at, at + size)
        sums = product(hidden, downs, cols).astype(jnp.bfloat16)
        for index, out in enumerate(outs):
            out[:, cols] = sums[index * each : (index + 1) * each]


def feed_half(feds, ups, downs, n_outs):
    rows = sum(fed.shape[0] for fed in feds)
    width, units = downs[0].shape[1], ups[0].shape[1]
    scoped = SCOPED if rows <= LANES else 32 << 20
    return pl.pallas_call(
        functools.partial(feed_kernel, len(feds), len(ups), len(downs), n_outs),
        out_shape=[jax.ShapeDtypeStruct((rows // n_outs, width), jnp.bfloat16)] * n_outs,
        in_specs=[IN_VMEM] * (len(feds) + len(ups) + len(downs)),
        out_specs=[IN_VMEM] * n_outs,
        scratch_shapes=[
            pltpu.VMEM((rows, width), jnp.bfloat16),
            pltpu.VMEM((rows, units), jnp.bfloat16),
        ],
        compiler_params=pltpu.CompilerParams(vmem_limit_bytes=scoped),
    )(*feds, *[in_vmem(part) for part in (*ups, *downs)])


def final_kernel(n_feeds, middle, *refs):
    feeds = refs[:n_feeds]
    mod, final_w, leaving_out, velocity = refs[n_feeds:]
    feed = feeds[0][...].astype(jnp.float32)
    for other in feeds[1:]:
        feed += other[...].astype(jnp.float32)
    leaving = middle[: feed.shape[0], :] + mod[5:6, :] * feed
    leaving_out[...] = leaving.astype(jnp.bfloat16)
    raw = lax.dot_general(
        modulated(leaving, mod, 6, 7),
        final_w[...],
        (((1,), (1,)), ((), ())),
        preferred_element_type=jnp.float32,
    )
    velocity[...] = jnp.concatenate([raw[at : at + 1, :] for at in range(raw.shape[0])], axis=1)


def final_step(middle, feeds, mod, final_w):
    rows, width = feeds[0].shape
    return pl.pallas_call(
        functools.partial(final_kernel, len(feeds)),
        out_shape=[
            jax.ShapeDtypeStruct((rows, width), jnp.bfloat16),
            jax.ShapeDtypeStruct((1, rows * final_w.shape[0]), jnp.float32),
        ],
        in_specs=[IN_VMEM] * (3 + len(feeds)),
        out_specs=[IN_VMEM] * 2,
        compiler_params=pltpu.CompilerParams(vmem_limit_bytes=SCOPED),
    )(middle, *feeds, mod, final_w)


def guided_kernel(raw, partner, latent, index, velocity, latent_next):
    position = index[...].astype(jnp.float32)
    step_size = noise_level(position + 1.0) - noise_level(position)
    is_guided = lax.axis_index("item") % 2 == 0
    guided = jnp.where(is_guided, raw[...], partner[...])
    unguided = jnp.where(is_guided, partner[...], raw[...])
    combined = unguided + GUIDANCE * (guided - unguided)
    velocity[...] = combined
    latent_next[...] = latent[...] + step_size * combined


def guided_step(raw, partner, latent, index):
    return pl.pallas_call(
        guided_kernel,
        out_shape=[jax.ShapeDtypeStruct(raw.shape, jnp.float32)] * 2,
        in_specs=[IN_VMEM] * 4,
        out_specs=[IN_VMEM] * 2,
        compiler_params=pltpu.CompilerParams(vmem_limit_bytes=SCOPED),
    )(raw, partner, latent, index)


def flipped(value, axes, mask, count):
    return lax.ppermute(value, axes, [(source, source ^ mask) for source in range(count)])


def on_device(
    tokens,
    text_keys_values,
    text_length,
    modulation,
    input_weight,
    norm_gain,
    output_weight,
    up_weight,
    down_weight,
    final_weight,
    step_index,
    latent,
):
    n_row, n_col = lax.axis_size("row"), lax.axis_size("col")
    width = tokens.shape[3]
    tile = tokens.reshape(-1, width)
    local = input_weight.shape[2]
    mod = modulation[0]
    in_w = input_weight.transpose(1, 0, 2).reshape(3 * width, local)
    paired = n_row == 2
    both = ("row", "col")
    count = n_row * n_col
    tile_rows = tile.shape[0]
    own_rows = n_row * tile_rows

    split = paired and n_col == 4
    shares = 2 if split else 1
    units = down_weight.shape[0] // shares
    up_parts = [(0, low, size, units) for low, size in spans(width, 3 * TILE)]
    thirds = [(0, part * width, width, local) for part in range(3)]
    step = max(LANES, units // 4 // TILE * TILE)
    down_parts = [(0, low, size, width) for low, size in spans(units, step)]
    if split:
        near = [tile] + [flipped(tile, both, mask, count) for mask in (n_col, 2, n_col + 2)]
        *in_ws, text = first_step(text_keys_values[0], in_w, thirds)
        *near, text = lax.optimization_barrier((*near, text))
        own_blocks = near[:2]
        normed = norm_step(near, mod)
        ready, far = [normed, flipped(normed, both, 1, count)], []
    else:
        gathered = lax.all_gather(tile, ("col", "row"), axis=0, tiled=True)
        far = [jnp.roll(gathered, -lax.axis_index("col") * own_rows, axis=0)]
        own_blocks = [far[0][:own_rows]]
        ready, normed = [], tile
        *in_ws, text = first_step(text_keys_values[0], in_w, thirds)
    mine = attention_half(
        ready,
        far,
        own_rows,
        text_length.reshape(1, 1),
        mod,
        norm_gain,
        text,
        in_ws,
        output_weight,
        normed,
    )
    if paired:
        theirs = flipped(mine, "row", 1, n_row)
    else:
        mine = lax.psum(mine.astype(jnp.float32), "row")
        theirs = mine
    *ups, done = fetch((up_weight,), up_parts, (mine,), shares)
    fed, middle = middle_step(own_blocks, mine, theirs, paired, mod, done)
    *downs, done = fetch((down_weight,), down_parts, (fed,), shares)
    if split:
        feds = [fed, flipped(fed, both, 1, count)]
        feed, *others = feed_half(feds, ups, downs, 4)
        feeds = [feed] + [
            flipped(part, both, mask, count) for part, mask in zip(others, (n_col, 1, n_col + 1))
        ]
    else:
        (feed,) = feed_half([fed], ups, downs, 1)
        if paired:
            feeds = [feed[:tile_rows], flipped(feed[tile_rows:], "row", 1, n_row)]
        else:
            feeds = [
                lax.psum_scatter(feed.astype(jnp.float32), "row", scatter_dimension=0, tiled=True)
            ]
            middle = lax.dynamic_slice_in_dim(
                middle, lax.axis_index("row") * tile_rows, tile_rows, 0
            )
    leaving, raw_velocity = final_step(middle, feeds, mod, final_weight.T)
    partner = flipped(raw_velocity, "item", 1, lax.axis_size("item"))
    velocity, latent_next = guided_step(
        raw_velocity, partner, latent.reshape(raw_velocity.shape), step_index.reshape(1, 1)
    )
    return (
        leaving.reshape(tokens.shape),
        velocity.reshape(latent.shape),
        latent_next.reshape(latent.shape),
    )


def solution(mesh):
    in_specs = (
        P("item", "row", "col", None),
        P("item", None, None, "row"),
        P("item"),
        P("item", None, None),
        P(None, None, "row"),
        P(),
        P("row", None),
        P(None, "row"),
        P("row", None),
        P(),
        P(),
        P("item", "row", "col"),
    )
    out_specs = (P("item", "row", "col", None), P("item", "row", "col"), P("item", "row", "col"))
    return jax.shard_map(
        on_device, mesh=mesh, in_specs=in_specs, out_specs=out_specs, check_vma=False
    )
```

```python
import functools

import jax
import jax.numpy as jnp
from jax import lax
from jax.experimental import pallas as pl
from jax.experimental.pallas import tpu as pltpu
from jax.sharding import PartitionSpec as P

HD = 64
STEPS = 28

EPSILON = 1e-06
SHIFT_FACTOR = 3.0
GUIDANCE = 4.5
MASKED = -1e30

LANES = 128
TILE = 256
ROWS = 16
SCOPED = 16 << 20
SCOPED_FETCH = 17 << 20

IN_VMEM = pl.BlockSpec(memory_space=pltpu.VMEM)
IN_PLACE = pl.BlockSpec(memory_space=pl.ANY)


def noise_level(position):
    linear = 1.0 - position / STEPS
    return SHIFT_FACTOR * linear / (1.0 + (SHIFT_FACTOR - 1.0) * linear)


def layer_norm(values):
    center = values - jnp.mean(values, axis=-1, keepdims=True)
    spread = jnp.mean(center * center, axis=-1, keepdims=True)
    return center * lax.rsqrt(spread + EPSILON)


def modulated(values, mod_ref, shift_row, scale_row):
    scale = 1.0 + mod_ref[scale_row : scale_row + 1, :]
    shift = mod_ref[shift_row : shift_row + 1, :]
    return (layer_norm(values) * scale + shift).astype(jnp.bfloat16)


def spans(width, step):
    return [(low, min(step, width - low)) for low in range(0, width, step)]


def for_rows(rows, step, body):
    if rows <= 2 * LANES:
        for low in range(0, rows, step):
            body(low)
    else:
        pl.loop(0, rows // step)(lambda at: body(pl.multiple_of(at * step, step)))


def in_hbm(array):
    return pltpu.with_memory_space_constraint(array, pltpu.HBM)


def in_vmem(array):
    return pltpu.with_memory_space_constraint(array, pltpu.VMEM)


def bytes_of(arrays):
    return sum(a.size * a.dtype.itemsize for a in arrays)


def copies_of(parts, sources, targets, sems, shares):
    share = lax.axis_index("col") % shares
    copies = []
    for index, ((at, low, rows, width), target) in enumerate(zip(parts, targets)):
        source = sources[at]
        if source.shape[1] == width:
            first = low + share * (source.shape[0] // shares)
            piece = source.at[pl.ds(pl.multiple_of(first, ROWS), rows)]
        else:
            piece = source.at[pl.ds(low, rows), pl.ds(pl.multiple_of(share * width, LANES), width)]
        copies.append(pltpu.make_async_copy(piece, target, sems.at[index]))
    return copies


def fetch_kernel(parts, shares, n_sources, n_after, *refs):
    sources, refs = refs[:n_sources], refs[n_sources + n_after :]
    targets, done, sems = refs[: len(parts)], refs[-2], refs[-1]
    copies = copies_of(parts, sources, targets, sems, shares)
    for copy in copies:
        copy.start()
    done[...] = jnp.zeros_like(done)
    for copy in copies:
        copy.wait()


def first_kernel(parts, text_hbm, source, *refs):
    *targets, split, text, text_sem, sems = refs
    text_copy = pltpu.make_async_copy(text_hbm, text, text_sem)
    text_copy.start()
    copies = copies_of(parts, (source,), targets, sems, 1)
    for copy in copies:
        copy.start()
    count = text.shape[0]
    split[...] = jnp.zeros_like(split)
    text_copy.wait()
    split[0, :count, :] = text[:, 0, :]
    split[1, :count, :] = text[:, 1, :]
    for copy in copies:
        copy.wait()


def first_step(text, source, parts):
    rows = -(-text.shape[0] // ROWS) * ROWS
    moved = sum(2 * size * width for at, low, size, width in parts)
    return pl.pallas_call(
        functools.partial(first_kernel, parts),
        out_shape=[pltpu.VMEM((size, width), jnp.bfloat16) for at, low, size, width in parts]
        + [jax.ShapeDtypeStruct((2, rows, text.shape[2]), jnp.bfloat16)],
        in_specs=[IN_PLACE] * 2,
        out_specs=[IN_VMEM] * (len(parts) + 1),
        scratch_shapes=[
            pltpu.VMEM(text.shape, jnp.bfloat16),
            pltpu.SemaphoreType.DMA,
            pltpu.SemaphoreType.DMA((len(parts),)),
        ],
        compiler_params=pltpu.CompilerParams(vmem_limit_bytes=SCOPED_FETCH),
        cost_estimate=pl.CostEstimate(flops=0, bytes_accessed=2 * moved, transcendentals=0),
    )(in_hbm(text), in_hbm(source))


def fetch(sources, parts, after=(), shares=1):
    shapes = [(rows, width) for at, low, rows, width in parts]
    moved = sum(2 * rows * width for rows, width in shapes)
    return pl.pallas_call(
        functools.partial(fetch_kernel, parts, shares, len(sources), len(after)),
        out_shape=[pltpu.VMEM(shape, jnp.bfloat16) for shape in shapes]
        + [jax.ShapeDtypeStruct((8, LANES), jnp.float32)],
        in_specs=[IN_PLACE] * (len(sources) + len(after)),
        out_specs=[IN_VMEM] * (len(parts) + 1),
        scratch_shapes=[pltpu.SemaphoreType.DMA((len(parts),))],
        compiler_params=pltpu.CompilerParams(vmem_limit_bytes=SCOPED_FETCH),
        cost_estimate=pl.CostEstimate(flops=0, bytes_accessed=2 * moved, transcendentals=0),
    )(*[in_hbm(source) for source in sources], *after)


def norm_kernel(n_blocks, *refs):
    blocks, mod, normed = refs[:n_blocks], refs[n_blocks], refs[-1]
    for at, block in enumerate(blocks):
        rows = block.shape[0]
        values = block[...].astype(jnp.float32)
        normed[at * rows : (at + 1) * rows, :] = modulated(values, mod, 0, 1)


def norm_step(blocks, mod):
    rows, width = sum(block.shape[0] for block in blocks), mod.shape[1]
    return pl.pallas_call(
        functools.partial(norm_kernel, len(blocks)),
        out_shape=jax.ShapeDtypeStruct((rows, width), jnp.bfloat16),
        in_specs=[IN_VMEM] * (len(blocks) + 1),
        out_specs=IN_VMEM,
        compiler_params=pltpu.CompilerParams(vmem_limit_bytes=SCOPED_FETCH),
        cost_estimate=pl.CostEstimate(
            flops=10 * rows * width, bytes_accessed=4 * rows * width, transcendentals=0
        ),
    )(*blocks, mod)


def attention_kernel(n_normed, n_blocks, own_rows, *refs):
    ready, refs = refs[:n_normed], refs[n_normed:]
    blocks = refs[:n_blocks]
    length, mod, gains, text, *in_ws, out_w = refs[n_blocks : n_blocks + 8]
    out, normed, q_ref, k_ref, v_ref, att_ref = refs[-6:]

    all_rows, width = normed.shape
    local = in_ws[0].shape[1]
    low = 0
    for part in ready:
        normed[low : low + part.shape[0], :] = part[...]
        low += part.shape[0]
    for block in blocks:

        def norm_rows(at, block=block, low=low):
            values = block[pl.ds(at, ROWS), :].astype(jnp.float32)
            normed[pl.ds(low + at, ROWS), :] = modulated(values, mod, 0, 1)

        for_rows(block.shape[0], ROWS, norm_rows)
        low += block.shape[0]

    tile = min(TILE, local)
    head_of_row = lax.broadcasted_iota(jnp.int32, (tile, tile), 0) // HD
    head_of_col = lax.broadcasted_iota(jnp.int32, (tile, tile), 1) // HD
    gain = jnp.concatenate([gains[...]] * (tile // HD), axis=1)
    same_head = (head_of_row == head_of_col).astype(jnp.bfloat16)

    def head_norm(values, part):
        squares = values * values
        high = squares.astype(jnp.bfloat16)
        total = jnp.dot(high, same_head, preferred_element_type=jnp.float32)
        if part == 0:
            rest = (squares - high.astype(jnp.float32)).astype(jnp.bfloat16)
            total += jnp.dot(rest, same_head, preferred_element_type=jnp.float32)
        gain_rows = gain[part : part + 1, :]
        return (values * lax.rsqrt(total * (1.0 / HD) + EPSILON) * gain_rows).astype(jnp.bfloat16)

    def project(first, rows, part, cols):
        return jnp.dot(
            normed[pl.ds(first, rows), :], in_ws[part][:, cols], preferred_element_type=jnp.float32
        )

    def project_rows(first, rows, part, target, columns):
        raws = [project(first, rows, part, cols) for cols in columns]
        normals = [head_norm(raw, part) for raw in raws]
        for cols, normal in zip(columns, normals):
            target[pl.ds(first, rows), cols] = normal

    columns = [slice(at, at + size) for at, size in spans(local, tile)]
    own_step, all_step = min(LANES, own_rows), min(LANES, all_rows)

    def keys_values(first):
        project_rows(first, all_step, 1, k_ref, columns)
        for cols in columns:
            values = project(first, all_step, 2, cols)
            v_ref[pl.ds(first, all_step), cols] = values.astype(jnp.bfloat16)

    for_rows(own_rows, own_step, lambda first: project_rows(first, own_step, 0, q_ref, columns))
    for_rows(all_rows, all_step, keys_values)

    used = lax.broadcasted_iota(jnp.int32, (1, text.shape[1]), 1) < length[...]
    first_head = lax.broadcasted_iota(jnp.int32, (1, LANES), 1) < HD
    contract = (((1,), (1,)), ((), ()))
    def attend(group):
        scores = []
        for cols in group:
            q = q_ref[:, cols]
            zero = jnp.zeros_like(q)
            pair = jnp.concatenate(
                [jnp.where(first_head, q, zero), jnp.where(first_head, zero, q)], 0
            )
            image = lax.dot_general(
                pair, k_ref[:, cols], contract, preferred_element_type=jnp.float32
            )
            other = lax.dot_general(
                pair, text[0, :, cols], contract, preferred_element_type=jnp.float32
            )
            scores.append(
                (HD ** (-0.5) * image, jnp.where(used, HD ** (-0.5) * other, MASKED))
            )
        largest = [
            jnp.maximum(
                jnp.max(image, axis=-1, keepdims=True), jnp.max(other, axis=-1, keepdims=True)
            )
            for image, other in scores
        ]
        weights = [
            (jnp.exp(image - top), jnp.exp(other - top))
            for (image, other), top in zip(scores, largest)
        ]
        totals = [
            jnp.sum(image, axis=-1, keepdims=True) + jnp.sum(other, axis=-1, keepdims=True)
            for image, other in weights
        ]
        for cols, (image, other), total in zip(group, weights, totals):
            mixed = jnp.dot(
                image.astype(jnp.bfloat16), v_ref[:, cols], preferred_element_type=jnp.float32
            )
            mixed += jnp.dot(
                other.astype(jnp.bfloat16), text[1, :, cols], preferred_element_type=jnp.float32
            )
            mixed = mixed / total
            att_ref[:, cols] = jnp.where(first_head, mixed[:own_rows], mixed[own_rows:]).astype(
                jnp.bfloat16
            )

    pairs = [slice(at, at + size) for at, size in spans(local, LANES)]
    group = len(pairs) if all_rows <= LANES else 1
    for first in range(0, len(pairs), group):
        attend(pairs[first : first + group])

    for at, size in spans(width, TILE):
        cols = slice(at, at + size)
        out[:, cols] = jnp.dot(
            att_ref[...], out_w[:, cols], preferred_element_type=jnp.float32
        ).astype(jnp.bfloat16)


def attention_half(ready, blocks, own_rows, length, mod, gains, text, in_ws, out_w, after):
    width, local = mod.shape[1], out_w.shape[0]
    all_rows = sum(part.shape[0] for part in (*ready, *blocks))
    scoped = SCOPED_FETCH if all_rows <= LANES else 48 << 20
    return pl.pallas_call(
        functools.partial(attention_kernel, len(ready), len(blocks), own_rows),
        out_shape=jax.ShapeDtypeStruct((own_rows, width), jnp.bfloat16),
        in_specs=[IN_VMEM] * (len(ready) + len(blocks)) + [IN_VMEM] * 8 + [IN_PLACE],
        out_specs=IN_VMEM,
        scratch_shapes=[
            pltpu.VMEM((all_rows, width), jnp.bfloat16),
            pltpu.VMEM((own_rows, local), jnp.bfloat16),
            pltpu.VMEM((all_rows, local), jnp.bfloat16),
            pltpu.VMEM((all_rows, local), jnp.bfloat16),
            pltpu.VMEM((own_rows, local), jnp.bfloat16),
        ],
        compiler_params=pltpu.CompilerParams(vmem_limit_bytes=scoped),
    )(
        *ready,
        *blocks,
        length,
        mod,
        gains,
        text,
        *[in_vmem(part) for part in in_ws],
        in_vmem(out_w),
        after,
    )


def middle_kernel(n_blocks, n_sums, paired, *refs):
    blocks, refs = refs[:n_blocks], refs[n_blocks:]
    sums, (mod, after, fed, middle) = refs[: 2 * n_sums], refs[2 * n_sums :]
    rows = sums[0].shape[0]
    tile = rows * n_sums // n_blocks
    step = tile if tile <= LANES else ROWS
    for at, block in enumerate(blocks):
        group, start = divmod(at * tile, rows)
        mine, theirs = sums[2 * group : 2 * group + 2]

        def norm_rows(low, at=at, block=block, start=start, mine=mine, theirs=theirs):
            here = pl.ds(at * tile + low, step)
            attention = mine[pl.ds(start + low, step), :].astype(jnp.float32)
            if paired:
                there = pl.ds((start + low + rows // 2) % rows, step)
                attention += theirs[there, :].astype(jnp.float32)
            values = block[pl.ds(low, step), :].astype(jnp.float32) + mod[2:3, :] * attention
            middle[here, :] = values
            fed[here, :] = modulated(values, mod, 3, 4)

        for_rows(tile, step, norm_rows)


def middle_step(blocks, sums, paired, mod, after):
    rows, width = sum(block.shape[0] for block in blocks), mod.shape[1]
    return pl.pallas_call(
        functools.partial(middle_kernel, len(blocks), len(sums) // 2, paired),
        out_shape=[
            jax.ShapeDtypeStruct((rows, width), jnp.bfloat16),
            jax.ShapeDtypeStruct((rows, width), jnp.float32),
        ],
        in_specs=[IN_VMEM] * (len(blocks) + len(sums) + 1) + [IN_PLACE],
        out_specs=[IN_VMEM] * 2,
        compiler_params=pltpu.CompilerParams(vmem_limit_bytes=SCOPED),
    )(*blocks, *sums, mod, after)


def feed_kernel(n_fed, n_ups, n_downs, n_outs, *refs):
    feds, refs = refs[:n_fed], refs[n_fed:]
    ups, refs = refs[:n_ups], refs[n_ups:]
    downs, outs = refs[:n_downs], refs[n_downs : n_downs + n_outs]
    fed, hidden = refs[-2:]
    rows, width = fed.shape
    units = hidden.shape[1]
    for at, part in enumerate(feds):
        fed[at * part.shape[0] : (at + 1) * part.shape[0], :] = part[...]

    def product(left, parts, cols):
        sums, low = 0.0, 0
        for part in parts:
            here = slice(low, low + part.shape[0])
            sums += jnp.dot(left[:, here], part[:, cols], preferred_element_type=jnp.float32)
            low = here.stop
        return sums

    for at, size in spans(units, TILE):
        cols = slice(at, at + size)
        hidden[:, cols] = jax.nn.gelu(product(fed, ups, cols), approximate=True).astype(jnp.bfloat16)

    each = rows // n_outs
    for at, size in spans(width, TILE):
        cols = slice(at, at + size)
        sums = product(hidden, downs, cols).astype(jnp.bfloat16)
        for index, out in enumerate(outs):
            out[:, cols] = sums[index * each : (index + 1) * each]


def feed_half(feds, ups, downs, n_outs):
    rows = sum(fed.shape[0] for fed in feds)
    width, units = downs[0].shape[1], ups[0].shape[1]
    scoped = SCOPED if rows <= LANES else 32 << 20
    return pl.pallas_call(
        functools.partial(feed_kernel, len(feds), len(ups), len(downs), n_outs),
        out_shape=[jax.ShapeDtypeStruct((rows // n_outs, width), jnp.bfloat16)] * n_outs,
        in_specs=[IN_VMEM] * (len(feds) + len(ups) + len(downs)),
        out_specs=[IN_VMEM] * n_outs,
        scratch_shapes=[
            pltpu.VMEM((rows, width), jnp.bfloat16),
            pltpu.VMEM((rows, units), jnp.bfloat16),
        ],
        compiler_params=pltpu.CompilerParams(vmem_limit_bytes=scoped),
    )(*feds, *[in_vmem(part) for part in (*ups, *downs)])


def final_kernel(n_feeds, middle, *refs):
    feeds = refs[:n_feeds]
    mod, final_w, leaving_out, velocity = refs[n_feeds:]
    feed = feeds[0][...].astype(jnp.float32)
    for other in feeds[1:]:
        feed += other[...].astype(jnp.float32)
    leaving = middle[: feed.shape[0], :] + mod[5:6, :] * feed
    leaving_out[...] = leaving.astype(jnp.bfloat16)
    raw = lax.dot_general(
        modulated(leaving, mod, 6, 7),
        final_w[...],
        (((1,), (1,)), ((), ())),
        preferred_element_type=jnp.float32,
    )
    velocity[...] = jnp.concatenate([raw[at : at + 1, :] for at in range(raw.shape[0])], axis=1)


def final_step(middle, feeds, mod, final_w):
    rows, width = feeds[0].shape
    return pl.pallas_call(
        functools.partial(final_kernel, len(feeds)),
        out_shape=[
            pltpu.VMEM((rows, width), jnp.bfloat16),
            jax.ShapeDtypeStruct((1, rows * final_w.shape[0]), jnp.float32),
        ],
        in_specs=[IN_VMEM] * (3 + len(feeds)),
        out_specs=[IN_VMEM] * 2,
        compiler_params=pltpu.CompilerParams(vmem_limit_bytes=SCOPED),
    )(middle, *feeds, mod, final_w)


def guided_kernel(raw, partner, latent, index, velocity, latent_next):
    position = index[...].astype(jnp.float32)
    step_size = noise_level(position + 1.0) - noise_level(position)
    is_guided = lax.axis_index("item") % 2 == 0
    guided = jnp.where(is_guided, raw[...], partner[...])
    unguided = jnp.where(is_guided, partner[...], raw[...])
    combined = unguided + GUIDANCE * (guided - unguided)
    velocity[...] = combined
    latent_next[...] = latent[...] + step_size * combined


def guided_step(raw, partner, latent, index):
    return pl.pallas_call(
        guided_kernel,
        out_shape=[jax.ShapeDtypeStruct(raw.shape, jnp.float32)] * 2,
        in_specs=[IN_VMEM] * 4,
        out_specs=[IN_VMEM] * 2,
        compiler_params=pltpu.CompilerParams(vmem_limit_bytes=SCOPED),
    )(raw, partner, latent, index)


def flipped(value, axes, mask, count):
    return lax.ppermute(value, axes, [(source, source ^ mask) for source in range(count)])


def on_device(
    tokens,
    text_keys_values,
    text_length,
    modulation,
    input_weight,
    norm_gain,
    output_weight,
    up_weight,
    down_weight,
    final_weight,
    step_index,
    latent,
):
    n_row, n_col = lax.axis_size("row"), lax.axis_size("col")
    width = tokens.shape[3]
    tile = tokens.reshape(-1, width)
    local = input_weight.shape[2]
    mod = modulation[0]
    in_w = input_weight.transpose(1, 0, 2).reshape(3 * width, local)
    paired = n_row == 2
    both = ("row", "col")
    count = n_row * n_col
    tile_rows = tile.shape[0]
    own_rows = n_row * tile_rows

    split = paired and n_col == 4
    shares = 2 if split else 1
    units = down_weight.shape[0] // shares
    up_parts = [(0, low, size, units) for low, size in spans(width, 3 * TILE)]
    thirds = [(0, part * width, width, local) for part in range(3)]
    step = max(LANES, units // 4 // TILE * TILE)
    down_parts = [(0, low, size, width) for low, size in spans(units, step)]
    if split:
        near = [tile] + [flipped(tile, both, mask, count) for mask in (n_col, 2, n_col + 2)]
        *in_ws, text = first_step(text_keys_values[0], in_w, thirds)
        *near, text = lax.optimization_barrier((*near, text))
        own_blocks = near[:2]
        normed = norm_step(near, mod)
        ready, far = [normed, flipped(normed, both, 1, count)], []
    else:
        gathered = lax.all_gather(tile, ("col", "row"), axis=0, tiled=True)
        far = [jnp.roll(gathered, -lax.axis_index("col") * own_rows, axis=0)]
        own_blocks = [far[0][:own_rows]]
        ready, normed = [], tile
        *in_ws, text = first_step(text_keys_values[0], in_w, thirds)
    mine = attention_half(
        ready,
        far,
        own_rows,
        text_length.reshape(1, 1),
        mod,
        norm_gain,
        text,
        in_ws,
        output_weight,
        normed,
    )
    if split:
        sums = [mine] + [flipped(mine, both, mask, count) for mask in (n_col, 1, n_col + 1)]
        own_blocks = own_blocks + [flipped(part, both, 1, count) for part in own_blocks]
    elif paired:
        sums = [mine, flipped(mine, "row", 1, n_row)]
    else:
        mine = lax.psum(mine.astype(jnp.float32), "row")
        sums = [mine, mine]
    weights = up_parts + [(1, *part[1:]) for part in down_parts]
    *fetched, done = fetch((up_weight, down_weight), weights, (mine,), shares)
    ups, downs = fetched[: len(up_parts)], fetched[len(up_parts) :]
    fed, middle = middle_step(own_blocks, sums, paired, mod, done)
    if split:
        feed, *others = feed_half([fed], ups, downs, 4)
        feeds = [feed]
        feeds.append(flipped(others[2], both, n_col + 1, count))
        feeds.append(flipped(others[0], both, n_col, count))
        feeds.append(flipped(others[1], both, 1, count))
    else:
        (feed,) = feed_half([fed], ups, downs, 1)
        if paired:
            feeds = [feed[:tile_rows], flipped(feed[tile_rows:], "row", 1, n_row)]
        else:
            feeds = [
                lax.psum_scatter(feed.astype(jnp.float32), "row", scatter_dimension=0, tiled=True)
            ]
            middle = lax.dynamic_slice_in_dim(
                middle, lax.axis_index("row") * tile_rows, tile_rows, 0
            )
    leaving, raw_velocity = final_step(middle, feeds, mod, final_weight.T)
    partner = flipped(raw_velocity, "item", 1, lax.axis_size("item"))
    velocity, latent_next = guided_step(
        raw_velocity, partner, latent.reshape(raw_velocity.shape), step_index.reshape(1, 1)
    )
    return (
        leaving.reshape(tokens.shape),
        velocity.reshape(latent.shape),
        latent_next.reshape(latent.shape),
    )


def solution(mesh):
    in_specs = (
        P("item", "row", "col", None),
        P("item", None, None, "row"),
        P("item"),
        P("item", None, None),
        P(None, None, "row"),
        P(),
        P("row", None),
        P(None, "row"),
        P("row", None),
        P(),
        P(),
        P("item", "row", "col"),
    )
    out_specs = (P("item", "row", "col", None), P("item", "row", "col"), P("item", "row", "col"))
    return jax.shard_map(
        on_device, mesh=mesh, in_specs=in_specs, out_specs=out_specs, check_vma=False
    )
```

```python
import functools

import jax
import jax.numpy as jnp
from jax import lax
from jax.experimental import pallas as pl
from jax.experimental.pallas import tpu as pltpu
from jax.sharding import PartitionSpec as P

HD = 64
STEPS = 28

EPSILON = 1e-06
SHIFT_FACTOR = 3.0
GUIDANCE = 4.5
MASKED = -1e30

LANES = 128
TILE = 256
ROWS = 16
SCOPED = 16 << 20
SCOPED_FETCH = 17 << 20

IN_VMEM = pl.BlockSpec(memory_space=pltpu.VMEM)
IN_PLACE = pl.BlockSpec(memory_space=pl.ANY)


def noise_level(position):
    linear = 1.0 - position / STEPS
    return SHIFT_FACTOR * linear / (1.0 + (SHIFT_FACTOR - 1.0) * linear)


def layer_norm(values):
    center = values - jnp.mean(values, axis=-1, keepdims=True)
    spread = jnp.mean(center * center, axis=-1, keepdims=True)
    return center * lax.rsqrt(spread + EPSILON)


def modulated(values, mod_ref, shift_row, scale_row):
    scale = 1.0 + mod_ref[scale_row : scale_row + 1, :]
    shift = mod_ref[shift_row : shift_row + 1, :]
    return (layer_norm(values) * scale + shift).astype(jnp.bfloat16)


def spans(width, step):
    return [(low, min(step, width - low)) for low in range(0, width, step)]


def for_rows(rows, step, body):
    if rows <= 2 * LANES:
        for low in range(0, rows, step):
            body(low)
    else:
        pl.loop(0, rows // step)(lambda at: body(pl.multiple_of(at * step, step)))


def in_hbm(array):
    return pltpu.with_memory_space_constraint(array, pltpu.HBM)


def in_vmem(array):
    return pltpu.with_memory_space_constraint(array, pltpu.VMEM)


def bytes_of(arrays):
    return sum(a.size * a.dtype.itemsize for a in arrays)


def copies_of(parts, sources, targets, sems, shares):
    share = lax.axis_index("col") % shares
    copies = []
    for index, ((at, low, rows, width), target) in enumerate(zip(parts, targets)):
        source = sources[at]
        if source.shape[1] == width:
            first = low + share * (source.shape[0] // shares)
            piece = source.at[pl.ds(pl.multiple_of(first, ROWS), rows)]
        else:
            piece = source.at[pl.ds(low, rows), pl.ds(pl.multiple_of(share * width, LANES), width)]
        copies.append(pltpu.make_async_copy(piece, target, sems.at[index]))
    return copies


def fetch_kernel(parts, shares, n_sources, n_after, *refs):
    sources, refs = refs[:n_sources], refs[n_sources + n_after :]
    targets, done, sems = refs[: len(parts)], refs[-2], refs[-1]
    copies = copies_of(parts, sources, targets, sems, shares)
    for copy in copies:
        copy.start()
    done[...] = jnp.zeros_like(done)
    for copy in copies:
        copy.wait()


def first_kernel(parts, text_hbm, source, *refs):
    *targets, split, text, text_sem, sems = refs
    text_copy = pltpu.make_async_copy(text_hbm, text, text_sem)
    text_copy.start()
    copies = copies_of(parts, (source,), targets, sems, 1)
    for copy in copies:
        copy.start()
    count = text.shape[0]
    split[...] = jnp.zeros_like(split)
    text_copy.wait()
    split[0, :count, :] = text[:, 0, :]
    split[1, :count, :] = text[:, 1, :]
    for copy in copies:
        copy.wait()


def first_step(text, source, parts):
    rows = -(-text.shape[0] // ROWS) * ROWS
    moved = sum(2 * size * width for at, low, size, width in parts)
    return pl.pallas_call(
        functools.partial(first_kernel, parts),
        out_shape=[pltpu.VMEM((size, width), jnp.bfloat16) for at, low, size, width in parts]
        + [jax.ShapeDtypeStruct((2, rows, text.shape[2]), jnp.bfloat16)],
        in_specs=[IN_PLACE] * 2,
        out_specs=[IN_VMEM] * (len(parts) + 1),
        scratch_shapes=[
            pltpu.VMEM(text.shape, jnp.bfloat16),
            pltpu.SemaphoreType.DMA,
            pltpu.SemaphoreType.DMA((len(parts),)),
        ],
        compiler_params=pltpu.CompilerParams(vmem_limit_bytes=SCOPED_FETCH),
        cost_estimate=pl.CostEstimate(flops=0, bytes_accessed=2 * moved, transcendentals=0),
    )(in_hbm(text), in_hbm(source))


def fetch(sources, parts, after=(), shares=1):
    shapes = [(rows, width) for at, low, rows, width in parts]
    moved = sum(2 * rows * width for rows, width in shapes)
    return pl.pallas_call(
        functools.partial(fetch_kernel, parts, shares, len(sources), len(after)),
        out_shape=[pltpu.VMEM(shape, jnp.bfloat16) for shape in shapes]
        + [jax.ShapeDtypeStruct((8, LANES), jnp.float32)],
        in_specs=[IN_PLACE] * (len(sources) + len(after)),
        out_specs=[IN_VMEM] * (len(parts) + 1),
        scratch_shapes=[pltpu.SemaphoreType.DMA((len(parts),))],
        compiler_params=pltpu.CompilerParams(vmem_limit_bytes=SCOPED_FETCH),
        cost_estimate=pl.CostEstimate(flops=0, bytes_accessed=2 * moved, transcendentals=0),
    )(*[in_hbm(source) for source in sources], *after)


def norm_kernel(n_blocks, *refs):
    blocks, mod, normed = refs[:n_blocks], refs[n_blocks], refs[-1]
    for at, block in enumerate(blocks):
        rows = block.shape[0]
        values = block[...].astype(jnp.float32)
        normed[at * rows : (at + 1) * rows, :] = modulated(values, mod, 0, 1)


def norm_step(blocks, mod):
    rows, width = sum(block.shape[0] for block in blocks), mod.shape[1]
    return pl.pallas_call(
        functools.partial(norm_kernel, len(blocks)),
        out_shape=jax.ShapeDtypeStruct((rows, width), jnp.bfloat16),
        in_specs=[IN_VMEM] * (len(blocks) + 1),
        out_specs=IN_VMEM,
        compiler_params=pltpu.CompilerParams(vmem_limit_bytes=SCOPED_FETCH),
        cost_estimate=pl.CostEstimate(
            flops=10 * rows * width, bytes_accessed=4 * rows * width, transcendentals=0
        ),
    )(*blocks, mod)


def attention_kernel(n_normed, n_blocks, own_rows, *refs):
    ready, refs = refs[:n_normed], refs[n_normed:]
    blocks = refs[:n_blocks]
    length, mod, gains, text, *in_ws, out_w = refs[n_blocks : n_blocks + 8]
    out, normed, q_ref, k_ref, v_ref, att_ref = refs[-6:]

    all_rows, width = normed.shape
    local = in_ws[0].shape[1]
    low = 0
    for part in ready:
        normed[low : low + part.shape[0], :] = part[...]
        low += part.shape[0]
    for block in blocks:

        def norm_rows(at, block=block, low=low):
            values = block[pl.ds(at, ROWS), :].astype(jnp.float32)
            normed[pl.ds(low + at, ROWS), :] = modulated(values, mod, 0, 1)

        for_rows(block.shape[0], ROWS, norm_rows)
        low += block.shape[0]

    tile = min(TILE, local)
    head_of_row = lax.broadcasted_iota(jnp.int32, (tile, tile), 0) // HD
    head_of_col = lax.broadcasted_iota(jnp.int32, (tile, tile), 1) // HD
    gain = jnp.concatenate([gains[...]] * (tile // HD), axis=1)
    same_head = (head_of_row == head_of_col).astype(jnp.bfloat16)

    def head_norm(values, part):
        squares = values * values
        high = squares.astype(jnp.bfloat16)
        total = jnp.dot(high, same_head, preferred_element_type=jnp.float32)
        if part == 0:
            rest = (squares - high.astype(jnp.float32)).astype(jnp.bfloat16)
            total += jnp.dot(rest, same_head, preferred_element_type=jnp.float32)
        gain_rows = gain[part : part + 1, :]
        return (values * lax.rsqrt(total * (1.0 / HD) + EPSILON) * gain_rows).astype(jnp.bfloat16)

    def project(first, rows, part, cols):
        return jnp.dot(
            normed[pl.ds(first, rows), :], in_ws[part][:, cols], preferred_element_type=jnp.float32
        )

    def project_rows(first, rows, part, target, columns):
        raws = [project(first, rows, part, cols) for cols in columns]
        normals = [head_norm(raw, part) for raw in raws]
        for cols, normal in zip(columns, normals):
            target[pl.ds(first, rows), cols] = normal

    columns = [slice(at, at + size) for at, size in spans(local, tile)]
    own_step, all_step = min(LANES, own_rows), min(LANES, all_rows)

    def keys_values(first):
        project_rows(first, all_step, 1, k_ref, columns)
        for cols in columns:
            values = project(first, all_step, 2, cols)
            v_ref[pl.ds(first, all_step), cols] = values.astype(jnp.bfloat16)

    for_rows(own_rows, own_step, lambda first: project_rows(first, own_step, 0, q_ref, columns))
    for_rows(all_rows, all_step, keys_values)

    used = lax.broadcasted_iota(jnp.int32, (1, text.shape[1]), 1) < length[...]
    first_head = lax.broadcasted_iota(jnp.int32, (1, LANES), 1) < HD
    contract = (((1,), (1,)), ((), ()))
    def attend(group):
        scores = []
        for cols in group:
            q = q_ref[:, cols]
            zero = jnp.zeros_like(q)
            pair = jnp.concatenate(
                [jnp.where(first_head, q, zero), jnp.where(first_head, zero, q)], 0
            )
            image = lax.dot_general(
                pair, k_ref[:, cols], contract, preferred_element_type=jnp.float32
            )
            other = lax.dot_general(
                pair, text[0, :, cols], contract, preferred_element_type=jnp.float32
            )
            scores.append(
                (HD ** (-0.5) * image, jnp.where(used, HD ** (-0.5) * other, MASKED))
            )
        largest = [
            jnp.maximum(
                jnp.max(image, axis=-1, keepdims=True), jnp.max(other, axis=-1, keepdims=True)
            )
            for image, other in scores
        ]
        weights = [
            (jnp.exp(image - top), jnp.exp(other - top))
            for (image, other), top in zip(scores, largest)
        ]
        totals = [
            jnp.sum(image, axis=-1, keepdims=True) + jnp.sum(other, axis=-1, keepdims=True)
            for image, other in weights
        ]
        for cols, (image, other), total in zip(group, weights, totals):
            mixed = jnp.dot(
                image.astype(jnp.bfloat16), v_ref[:, cols], preferred_element_type=jnp.float32
            )
            mixed += jnp.dot(
                other.astype(jnp.bfloat16), text[1, :, cols], preferred_element_type=jnp.float32
            )
            mixed = mixed / total
            att_ref[:, cols] = jnp.where(first_head, mixed[:own_rows], mixed[own_rows:]).astype(
                jnp.bfloat16
            )

    pairs = [slice(at, at + size) for at, size in spans(local, LANES)]
    group = len(pairs) if all_rows <= LANES else 1
    for first in range(0, len(pairs), group):
        attend(pairs[first : first + group])

    for at, size in spans(width, TILE):
        cols = slice(at, at + size)
        out[:, cols] = jnp.dot(
            att_ref[...], out_w[:, cols], preferred_element_type=jnp.float32
        ).astype(jnp.bfloat16)


def attention_half(ready, blocks, own_rows, length, mod, gains, text, in_ws, out_w, after):
    width, local = mod.shape[1], out_w.shape[0]
    all_rows = sum(part.shape[0] for part in (*ready, *blocks))
    scoped = SCOPED_FETCH if all_rows <= LANES else 48 << 20
    return pl.pallas_call(
        functools.partial(attention_kernel, len(ready), len(blocks), own_rows),
        out_shape=jax.ShapeDtypeStruct((own_rows, width), jnp.bfloat16),
        in_specs=[IN_VMEM] * (len(ready) + len(blocks)) + [IN_VMEM] * 8 + [IN_PLACE] * len(after),
        out_specs=IN_VMEM,
        scratch_shapes=[
            pltpu.VMEM((all_rows, width), jnp.bfloat16),
            pltpu.VMEM((own_rows, local), jnp.bfloat16),
            pltpu.VMEM((all_rows, local), jnp.bfloat16),
            pltpu.VMEM((all_rows, local), jnp.bfloat16),
            pltpu.VMEM((own_rows, local), jnp.bfloat16),
        ],
        compiler_params=pltpu.CompilerParams(vmem_limit_bytes=scoped),
    )(
        *ready,
        *blocks,
        length,
        mod,
        gains,
        text,
        *[in_vmem(part) for part in in_ws],
        in_vmem(out_w),
        *after,
    )


def middle_kernel(n_blocks, n_sums, paired, *refs):
    blocks, refs = refs[:n_blocks], refs[n_blocks:]
    sums, (mod, after, fed, middle) = refs[: 2 * n_sums], refs[2 * n_sums :]
    rows = sums[0].shape[0]
    tile = rows * n_sums // n_blocks
    step = tile if tile <= LANES else ROWS
    for at, block in enumerate(blocks):
        group, start = divmod(at * tile, rows)
        mine, theirs = sums[2 * group : 2 * group + 2]

        def norm_rows(low, at=at, block=block, start=start, mine=mine, theirs=theirs):
            here = pl.ds(at * tile + low, step)
            attention = mine[pl.ds(start + low, step), :].astype(jnp.float32)
            if paired:
                there = pl.ds((start + low + rows // 2) % rows, step)
                attention += theirs[there, :].astype(jnp.float32)
            values = block[pl.ds(low, step), :].astype(jnp.float32) + mod[2:3, :] * attention
            middle[here, :] = values
            fed[here, :] = modulated(values, mod, 3, 4)

        for_rows(tile, step, norm_rows)


def middle_step(blocks, sums, paired, mod, after):
    rows, width = sum(block.shape[0] for block in blocks), mod.shape[1]
    return pl.pallas_call(
        functools.partial(middle_kernel, len(blocks), len(sums) // 2, paired),
        out_shape=[
            jax.ShapeDtypeStruct((rows, width), jnp.bfloat16),
            jax.ShapeDtypeStruct((rows, width), jnp.float32),
        ],
        in_specs=[IN_VMEM] * (len(blocks) + len(sums) + 1) + [IN_PLACE],
        out_specs=[IN_VMEM] * 2,
        compiler_params=pltpu.CompilerParams(vmem_limit_bytes=SCOPED),
    )(*blocks, *sums, mod, after)


def feed_kernel(n_fed, n_ups, n_downs, n_outs, *refs):
    feds, refs = refs[:n_fed], refs[n_fed:]
    ups, refs = refs[:n_ups], refs[n_ups:]
    downs, outs = refs[:n_downs], refs[n_downs : n_downs + n_outs]
    fed, hidden = refs[-2:]
    rows, width = fed.shape
    units = hidden.shape[1]
    for at, part in enumerate(feds):
        fed[at * part.shape[0] : (at + 1) * part.shape[0], :] = part[...]

    def product(left, parts, cols):
        sums, low = 0.0, 0
        for part in parts:
            here = slice(low, low + part.shape[0])
            sums += jnp.dot(left[:, here], part[:, cols], preferred_element_type=jnp.float32)
            low = here.stop
        return sums

    for at, size in spans(units, TILE):
        cols = slice(at, at + size)
        hidden[:, cols] = jax.nn.gelu(product(fed, ups, cols), approximate=True).astype(jnp.bfloat16)

    each = rows // n_outs
    for at, size in spans(width, TILE):
        cols = slice(at, at + size)
        sums = product(hidden, downs, cols).astype(jnp.bfloat16)
        for index, out in enumerate(outs):
            out[:, cols] = sums[index * each : (index + 1) * each]


def feed_half(feds, ups, downs, n_outs):
    rows = sum(fed.shape[0] for fed in feds)
    width, units = downs[0].shape[1], ups[0].shape[1]
    scoped = SCOPED if rows <= LANES else 32 << 20
    return pl.pallas_call(
        functools.partial(feed_kernel, len(feds), len(ups), len(downs), n_outs),
        out_shape=[jax.ShapeDtypeStruct((rows // n_outs, width), jnp.bfloat16)] * n_outs,
        in_specs=[IN_VMEM] * (len(feds) + len(ups) + len(downs)),
        out_specs=[IN_VMEM] * n_outs,
        scratch_shapes=[
            pltpu.VMEM((rows, width), jnp.bfloat16),
            pltpu.VMEM((rows, units), jnp.bfloat16),
        ],
        compiler_params=pltpu.CompilerParams(vmem_limit_bytes=scoped),
    )(*feds, *[in_vmem(part) for part in (*ups, *downs)])


def final_kernel(n_feeds, middle, *refs):
    feeds = refs[:n_feeds]
    mod, final_w, leaving_out, velocity = refs[n_feeds:]
    feed = feeds[0][...].astype(jnp.float32)
    for other in feeds[1:]:
        feed += other[...].astype(jnp.float32)
    leaving = middle[: feed.shape[0], :] + mod[5:6, :] * feed
    leaving_out[...] = leaving.astype(jnp.bfloat16)
    raw = lax.dot_general(
        modulated(leaving, mod, 6, 7),
        final_w[...],
        (((1,), (1,)), ((), ())),
        preferred_element_type=jnp.float32,
    )
    velocity[...] = jnp.concatenate([raw[at : at + 1, :] for at in range(raw.shape[0])], axis=1)


def final_step(middle, feeds, mod, final_w):
    rows, width = feeds[0].shape
    return pl.pallas_call(
        functools.partial(final_kernel, len(feeds)),
        out_shape=[
            pltpu.VMEM((rows, width), jnp.bfloat16),
            jax.ShapeDtypeStruct((1, rows * final_w.shape[0]), jnp.float32),
        ],
        in_specs=[IN_VMEM] * (3 + len(feeds)),
        out_specs=[IN_VMEM] * 2,
        compiler_params=pltpu.CompilerParams(vmem_limit_bytes=SCOPED),
    )(middle, *feeds, mod, final_w)


def guided_kernel(raw, partner, latent, index, velocity, latent_next):
    position = index[...].astype(jnp.float32)
    step_size = noise_level(position + 1.0) - noise_level(position)
    is_guided = lax.axis_index("item") % 2 == 0
    guided = jnp.where(is_guided, raw[...], partner[...])
    unguided = jnp.where(is_guided, partner[...], raw[...])
    combined = unguided + GUIDANCE * (guided - unguided)
    velocity[...] = combined
    latent_next[...] = latent[...] + step_size * combined


def guided_step(raw, partner, latent, index):
    return pl.pallas_call(
        guided_kernel,
        out_shape=[jax.ShapeDtypeStruct(raw.shape, jnp.float32)] * 2,
        in_specs=[IN_VMEM] * 4,
        out_specs=[IN_VMEM] * 2,
        compiler_params=pltpu.CompilerParams(vmem_limit_bytes=SCOPED),
    )(raw, partner, latent, index)


def flipped(value, axes, mask, count):
    return lax.ppermute(value, axes, [(source, source ^ mask) for source in range(count)])


def on_device(
    tokens,
    text_keys_values,
    text_length,
    modulation,
    input_weight,
    norm_gain,
    output_weight,
    up_weight,
    down_weight,
    final_weight,
    step_index,
    latent,
):
    n_row, n_col = lax.axis_size("row"), lax.axis_size("col")
    width = tokens.shape[3]
    tile = tokens.reshape(-1, width)
    local = input_weight.shape[2]
    mod = modulation[0]
    in_w = input_weight.transpose(1, 0, 2).reshape(3 * width, local)
    paired = n_row == 2
    both = ("row", "col")
    count = n_row * n_col
    tile_rows = tile.shape[0]
    own_rows = n_row * tile_rows

    split = paired and n_col == 4
    shares = 2 if split else 1
    units = down_weight.shape[0] // shares
    up_parts = [(0, low, size, units) for low, size in spans(width, 3 * TILE)]
    thirds = [(0, part * width, width, local) for part in range(3)]
    step = max(LANES, units // 4 // TILE * TILE)
    down_parts = [(0, low, size, width) for low, size in spans(units, step)]
    if split:
        near = [tile] + [flipped(tile, both, mask, count) for mask in (n_col, 2, n_col + 2)]
        *in_ws, text = first_step(text_keys_values[0], in_w, thirds)
        *near, text = lax.optimization_barrier((*near, text))
        own_blocks = near[:2]
        normed = norm_step(near, mod)
        ready, far = [normed, flipped(normed, both, 1, count)], []
        peer_blocks = [flipped(part, both, 1, count) for part in own_blocks]
    else:
        gathered = lax.all_gather(tile, ("col", "row"), axis=0, tiled=True)
        far = [jnp.roll(gathered, -lax.axis_index("col") * own_rows, axis=0)]
        own_blocks = [far[0][:own_rows]]
        ready, normed, peer_blocks = [], tile, []
        *in_ws, text = first_step(text_keys_values[0], in_w, thirds)
    mine = attention_half(
        ready,
        far,
        own_rows,
        text_length.reshape(1, 1),
        mod,
        norm_gain,
        text,
        in_ws,
        output_weight,
        (normed, *peer_blocks),
    )
    if split:
        sums = [mine] + [flipped(mine, both, mask, count) for mask in (n_col, 1, n_col + 1)]
        own_blocks = own_blocks + peer_blocks
    elif paired:
        sums = [mine, flipped(mine, "row", 1, n_row)]
    else:
        mine = lax.psum(mine.astype(jnp.float32), "row")
        sums = [mine, mine]
    weights = up_parts + [(1, *part[1:]) for part in down_parts]
    *fetched, done = fetch((up_weight, down_weight), weights, (mine,), shares)
    ups, downs = fetched[: len(up_parts)], fetched[len(up_parts) :]
    fed, middle = middle_step(own_blocks, sums, paired, mod, done)
    if split:
        feed, *others = feed_half([fed], ups, downs, 4)
        feeds = [feed]
        feeds.append(flipped(others[2], both, n_col + 1, count))
        feeds.append(flipped(others[0], both, n_col, count))
        feeds.append(flipped(others[1], both, 1, count))
    else:
        (feed,) = feed_half([fed], ups, downs, 1)
        if paired:
            feeds = [feed[:tile_rows], flipped(feed[tile_rows:], "row", 1, n_row)]
        else:
            feeds = [
                lax.psum_scatter(feed.astype(jnp.float32), "row", scatter_dimension=0, tiled=True)
            ]
            middle = lax.dynamic_slice_in_dim(
                middle, lax.axis_index("row") * tile_rows, tile_rows, 0
            )
    leaving, raw_velocity = final_step(middle, feeds, mod, final_weight.T)
    partner = flipped(raw_velocity, "item", 1, lax.axis_size("item"))
    velocity, latent_next = guided_step(
        raw_velocity, partner, latent.reshape(raw_velocity.shape), step_index.reshape(1, 1)
    )
    return (
        leaving.reshape(tokens.shape),
        velocity.reshape(latent.shape),
        latent_next.reshape(latent.shape),
    )


def solution(mesh):
    in_specs = (
        P("item", "row", "col", None),
        P("item", None, None, "row"),
        P("item"),
        P("item", None, None),
        P(None, None, "row"),
        P(),
        P("row", None),
        P(None, "row"),
        P("row", None),
        P(),
        P(),
        P("item", "row", "col"),
    )
    out_specs = (P("item", "row", "col", None), P("item", "row", "col"), P("item", "row", "col"))
    return jax.shard_map(
        on_device, mesh=mesh, in_specs=in_specs, out_specs=out_specs, check_vma=False
    )
```
